512 devices in a mesh: row: 32 (over x, z), col: 16 (over y, core).
Axes of the slice: x: 4, y: 8, z: 8, core: 2. Of those that a mesh axis runs over, the one named last changes fastest.
Arguments:
- charges: bfloat16 [64, 64, 64, 512], P('row', 'col'), may hold values from -6 to 6
- offsets: bfloat16 [64, 64, 3, 512], P('row', 'col'), may hold values from 0 to 1
- leaf_basis: bfloat16 [64, 64, 64, 512], P('row', 'col'), may hold values from -0.25 to 0.25
- near_mask: int32 [64, 64, 8], P('row', 'col'), may hold values 0 or 1
- leaf_coupling: bfloat16 [64, 64, 64, 1600], P('row', 'col'), may hold values from -0.15625 to 0.15625
- leaf_distant_flags: int32 [64, 64, 25], P('row', 'col'), may hold values 0 or 1
- leaf_transfer: bfloat16 [64, 64, 64, 64], P('row', 'col'), may hold values from -0.25 to 0.25
- box_coupling: bfloat16 [32, 16, 3, 64, 1600], P('row', 'col'), may hold values from -0.15625 to 0.15625
- box_far: int32 [32, 16, 3, 25], P('row', 'col'), may hold values 0 or 1
- parent_child_transfer: bfloat16 [32, 16, 2, 64, 64], P('row', 'col'), may hold values from -0.375 to 0.375
Outputs:
- potential: bfloat16 [64, 64, 64, 512], P('row', 'col')
The draws below stay inside these ranges and needn't reach their ends.
All inputs are finite; a program needn't handle non-finite values. No bound on the sum of `near_mask` or of `leaf_distant_flags` or of `box_far` on one device may be relied on, other than what follows from the above.
Results may differ from the reference program's by a relative error of at most 0.0049.
Values may be sent and summed in bfloat16 or wider, within the bound.
No kernel may reach another device: no remote copies, remote signals or barrier semaphores. Data moves between devices by JAX's collectives and lax.ppermute only.
A program may use at most 128 MiB of HBM per device.

```python
import math
import jax
import jax.numpy as jnp
from jax import lax

PANELS = 512
RANK = 64
LOADS = 64
LEAF_ROWS = 2
LEAF_COLS = 4
BOX_OFFSETS = 25
LEAF_GRID_ROWS = 64
LEAF_GRID_COLS = 64
N_ROW = 32
N_COL = 16


def set_ends(array, key, least, largest):
    longest = array.shape.index(max(array.shape))
    spots = []
    for shift in (0, 1):
        where = [jax.random.randint(jax.random.fold_in(key, axis), (), 0, length) for axis, length in enumerate(array.shape)]
        where[longest] = (where[longest] + shift) % array.shape[longest]
        spots.append(tuple(where))
    return array.at[spots[0]].set(least).at[spots[1]].set(largest)


def shard_levels(own_key, shape, shards, least, high):
    level, own = 1.0, jax.random.fold_in(own_key, 6)
    for axis_at, blocks in shards:
        draws = jnp.exp(jax.random.uniform(jax.random.fold_in(own, axis_at), (blocks,), jnp.float32, least / len(shards), high / len(shards)))
        level = level * jnp.repeat(draws, shape[axis_at] // blocks).reshape([-1 if axis == axis_at else 1 for axis in range(len(shape))])
    return level


def noise(key, extent, scale, bound, cuts=(), kind=jnp.bfloat16):
    loudness = shard_levels(key, extent, cuts, -0.22, 0.18) if cuts else 1.0
    array = jax.random.normal(key, extent, jnp.float32) * scale * loudness
    return jnp.minimum(jnp.maximum(array, -bound), bound).astype(kind)


def setup_inputs(seed: int = 0) -> dict:
    seeds = jax.random.split(jax.random.key(seed), 11)
    return {
        "charges": noise(seeds[0], (LEAF_GRID_ROWS, LEAF_GRID_COLS, LOADS, PANELS), 1.0, 6.0, ((0, 32), (1, 16))),
        "offsets": jnp.clip(1.0 * jax.random.uniform(seeds[1], (LEAF_GRID_ROWS, LEAF_GRID_COLS, 3, PANELS), jnp.float32) ** shard_levels(seeds[1], (LEAF_GRID_ROWS, LEAF_GRID_COLS, 3, PANELS), ((0, 32), (1, 16)), -0.2, 0.2), 0.0, 1.0).astype(jnp.bfloat16),
        "leaf_basis": noise(seeds[2], (LEAF_GRID_ROWS, LEAF_GRID_COLS, RANK, PANELS), PANELS ** -0.5, 0.25, ((0, 32), (1, 16))),
        "near_mask": set_ends((jax.random.randint(seeds[3], (LEAF_GRID_ROWS, LEAF_GRID_COLS, 8), 0, 2) < 1).astype(jnp.int32), jax.random.fold_in(seeds[3], 1), 0, 1),
        "leaf_coupling": noise(seeds[4], (LEAF_GRID_ROWS, LEAF_GRID_COLS, RANK, BOX_OFFSETS * RANK), (RANK * 19) ** -0.5, 0.15625, ((0, 32), (1, 16))),
        "leaf_distant_flags": set_ends((jax.random.randint(seeds[5], (LEAF_GRID_ROWS, LEAF_GRID_COLS, BOX_OFFSETS), 0, 4) < 3).astype(jnp.int32), jax.random.fold_in(seeds[5], 1), 0, 1),
        "leaf_transfer": noise(seeds[6], (LEAF_GRID_ROWS, LEAF_GRID_COLS, RANK, RANK), (RANK * LEAF_ROWS * LEAF_COLS) ** -0.5, 0.25, ((0, 32), (1, 16))),
        "box_coupling": noise(seeds[7], (N_ROW, N_COL, 3, RANK, BOX_OFFSETS * RANK), (RANK * 19) ** -0.5, 0.15625, ((0, 32), (1, 16))),
        "box_far": set_ends((jax.random.randint(seeds[8], (N_ROW, N_COL, 3, BOX_OFFSETS), 0, 4) < 3).astype(jnp.int32), jax.random.fold_in(seeds[8], 1), 0, 1),
        "parent_child_transfer": noise(seeds[9], (N_ROW, N_COL, 2, RANK, RANK), (RANK * 4) ** -0.5, 0.375, ((0, 32), (1, 16))),
    }


EPSILON = 0.001

def near_tile(source_off, target_off, row_off, col_off, factor):
    source = source_off.astype(jnp.float32)
    target = target_off.astype(jnp.float32)
    delta_x = (col_off + source[0])[:, None] - target[0][None, :]
    delta_y = (row_off + source[1])[:, None] - target[1][None, :]
    delta_z = source[2][:, None] - target[2][None, :]
    squared = delta_x * delta_x + delta_y * delta_y + delta_z * delta_z + EPSILON
    return (lax.rsqrt(squared) * factor).astype(jnp.bfloat16)

def near_weights(near_mask):
    flags = near_mask.astype(jnp.float32)
    center = jnp.ones(flags.shape[:-1] + (1,), jnp.float32)
    return jnp.concatenate([flags[..., :4], center, flags[..., 4:]], axis=-1)

def box_level(box_grid, group, coupling, flags):
    padded = jnp.pad(box_grid, ((2, 2), (2, 2), (0, 0), (0, 0)))
    lattice_rows = box_grid.shape[0]
    grid_cols = box_grid.shape[1]
    summed = jnp.zeros((N_ROW, N_COL, RANK, LOADS), jnp.float32)
    for place in range(25):
        row_off = place // 5 - 2
        col_off = place % 5 - 2
        window = padded[2 + row_off:2 + row_off + lattice_rows, 2 + col_off:2 + col_off + grid_cols]
        window = jnp.repeat(jnp.repeat(window, group, axis=0), group, axis=1)
        window = window * flags[:, :, place][:, :, None, None].astype(jnp.bfloat16)
        matrix = coupling[:, :, :, place * RANK:(place + 1) * RANK]
        summed = summed + jnp.einsum('ijkm,ijmr->ijkr', matrix.astype(jnp.float32), window.astype(jnp.float32))
    return summed

def reference(charges, offsets, leaf_basis, near_mask, leaf_coupling, leaf_distant_flags, leaf_transfer, box_coupling, box_far, parent_child_transfer):
    lattice_rows = LEAF_GRID_ROWS
    grid_cols = LEAF_GRID_COLS
    factor = 1.0 / math.sqrt(PANELS)
    pad_charges = jnp.pad(charges, ((1, 1), (1, 1), (0, 0), (0, 0)))
    pad_offsets = jnp.pad(offsets, ((1, 1), (1, 1), (0, 0), (0, 0)))
    weights = near_weights(near_mask)
    tiles_of = jax.vmap(near_tile, in_axes=(0, 0, None, None, None))

    def near_row(row_index):
        block_charges = lax.dynamic_slice_in_dim(pad_charges, row_index, 3, 0)
        block_shift_table = lax.dynamic_slice_in_dim(pad_offsets, row_index, 3, 0)
        target = lax.dynamic_slice_in_dim(offsets, row_index, 1, 0)[0]
        row_weights = lax.dynamic_slice_in_dim(weights, row_index, 1, 0)[0]
        summed = jnp.zeros((grid_cols, LOADS, PANELS), jnp.float32)
        for slot in range(9):
            row_off = slot // 3 - 1
            col_off = slot % 3 - 1
            source_charges = block_charges[row_off + 1, 1 + col_off:1 + col_off + grid_cols]
            source_offsets = block_shift_table[row_off + 1, 1 + col_off:1 + col_off + grid_cols]
            kernel_tile = tiles_of(source_offsets, target, row_off, col_off, factor)
            product = jnp.einsum('nrs,nst->nrt', source_charges.astype(jnp.float32), kernel_tile.astype(jnp.float32))
            summed = summed + product * row_weights[:, slot][:, None, None]
        return summed
    near_field = lax.map(near_row, jnp.arange(lattice_rows, dtype=jnp.int32))

    def multipole_row(row_items):
        basis_row, source_charge_row = row_items
        product = jnp.einsum('nkp,nrp->nkr', basis_row.astype(jnp.float32), source_charge_row.astype(jnp.float32))
        return product.astype(jnp.bfloat16)
    multipoles = lax.map(multipole_row, (leaf_basis, charges))
    flat_poles = multipoles.reshape(lattice_rows, grid_cols, RANK * LOADS)
    padded = jnp.pad(flat_poles, ((2, 2), (2, 2), (0, 0)))
    leaf_local = jnp.zeros((lattice_rows, grid_cols, RANK, LOADS), jnp.float32)
    for place in range(25):
        row_off = place // 5 - 2
        col_off = place % 5 - 2
        window = padded[2 + row_off:2 + row_off + lattice_rows, 2 + col_off:2 + col_off + grid_cols]
        window = window * leaf_distant_flags[:, :, place][:, :, None].astype(jnp.bfloat16)
        window = window.reshape(lattice_rows, grid_cols, RANK, LOADS)
        matrix = leaf_coupling[:, :, :, place * RANK:(place + 1) * RANK]
        leaf_local = leaf_local + jnp.einsum('abkj,abjr->abkr', matrix.astype(jnp.float32), window.astype(jnp.float32))
    transfer_blocks = leaf_transfer.reshape(N_ROW, LEAF_ROWS, N_COL, LEAF_COLS, RANK, RANK)
    pole_blocks = multipoles.reshape(N_ROW, LEAF_ROWS, N_COL, LEAF_COLS, RANK, LOADS)
    coarse_box_one = jnp.einsum('iajbkm,iajbkr->ijmr', transfer_blocks.astype(jnp.float32), pole_blocks.astype(jnp.float32)).astype(jnp.bfloat16)
    level_terms = jnp.einsum('ijxkm,ijkr->ijxmr', parent_child_transfer.astype(jnp.float32), coarse_box_one.astype(jnp.float32)).astype(jnp.bfloat16)
    second = level_terms[:, :, 0].astype(jnp.float32).reshape(N_ROW // 2, 2, N_COL // 2, 2, RANK, LOADS)
    box2 = second.sum(axis=(1, 3)).astype(jnp.bfloat16)
    third = level_terms[:, :, 1].astype(jnp.float32).reshape(N_ROW // 4, 4, N_COL // 4, 4, RANK, LOADS)
    box3 = third.sum(axis=(1, 3)).astype(jnp.bfloat16)
    box_local = box_level(coarse_box_one, 1, box_coupling[:, :, 0], box_far[:, :, 0])
    box_local = box_local + box_level(box2, 2, box_coupling[:, :, 1], box_far[:, :, 1])
    box_local = box_local + box_level(box3, 4, box_coupling[:, :, 2], box_far[:, :, 2])
    box_local = box_local.astype(jnp.bfloat16)
    spread = jnp.repeat(jnp.repeat(box_local, LEAF_ROWS, axis=0), LEAF_COLS, axis=1)
    local = leaf_local + jnp.einsum('abkj,abjr->abkr', leaf_transfer.astype(jnp.float32), spread.astype(jnp.float32))
    local = local.astype(jnp.bfloat16)

    def finish_row(row_items):
        near_row_field, local_row, basis_row = row_items
        far_part = jnp.einsum('nkr,nkp->nrp', local_row.astype(jnp.float32), basis_row.astype(jnp.float32))
        return (near_row_field + far_part).astype(jnp.bfloat16)
    return lax.map(finish_row, (near_field, local, leaf_basis))
```

```python
import functools

import jax
import jax.numpy as jnp
from jax import lax
from jax.experimental import pallas as pl
from jax.experimental.pallas import tpu as pltpu
from jax.sharding import PartitionSpec as P

PANELS = 512
RANK = 64
LOADS = 64
EPSILON = 0.001
F32 = jnp.float32
BF16 = jnp.bfloat16
NT = (((1,), (1,)), ((), ()))
TN = (((0,), (0,)), ((), ()))
WIDE = 25 * RANK
MIB = 2**20
VMEM = pl.BlockSpec(memory_space=pltpu.VMEM)
SMEM = pl.BlockSpec(memory_space=pltpu.SMEM)

ROW_OFFS, ROW_POLES, ROW_BOX, ROW_ALL = 256, 272, 336, 352
COL_OFFS, COL_POLES, COL_BOX, COL_ALL = 256, 272, 368, 416


def shifted(value, axis, steps):
    count = lax.axis_size(axis)
    initial, last = (max(0, -steps), min(count, count - steps))
    return lax.ppermute(value, axis, [(source, source + steps) for source in range(initial, last)])


def swapped(value, axis, bit):
    return lax.ppermute(value, axis, [(i, i ^ 1 << bit) for i in range(lax.axis_size(axis))])


def kernel_call(body, outs, scratch, name, cost, *args, smem=()):
    return pl.pallas_call(
        body,
        out_shape=outs,
        in_specs=[SMEM if i in smem else VMEM for i in range(len(args))],
        out_specs=jax.tree.map(lambda _: VMEM, outs),
        scratch_shapes=scratch,
        compiler_params=pltpu.CompilerParams(vmem_limit_bytes=40 * MIB),
        cost_estimate=pl.CostEstimate(flops=cost, bytes_accessed=4 * MIB, transcendentals=0),
        name=name,
    )(*args)


def shape(dims, dtype=BF16):
    return jax.ShapeDtypeStruct(dims, dtype)


def fold(matrix):
    return jnp.concatenate([matrix[:32], matrix[32:]], axis=1)


def unfold(folded):
    return jnp.concatenate([folded[:, :64], folded[:, 64:]], axis=0)


def flat(folded):
    return jnp.concatenate([folded[:16], folded[16:]], axis=1)


def unflat(flattened):
    return jnp.concatenate([flattened[:, :128], flattened[:, 128:]], axis=0)


def rows_of(values, count):
    row = lax.broadcasted_iota(jnp.int32, (count, PANELS), 0)
    out = jnp.zeros((count, PANELS), F32)
    for index, value in enumerate(values):
        out = jnp.where(row == index, value, out)
    return out


def three_parts(value):
    high = value.astype(BF16).astype(F32)
    rest = value - high
    middle = rest.astype(BF16).astype(F32)
    low = (rest - middle).astype(BF16).astype(F32)
    return high, middle, low


def target_features(off):
    x, y, z = off[0:1], off[1:2], off[2:3]
    high, middle, low = three_parts(PANELS * (x * x + y * y + z * z + EPSILON))
    return rows_of([x, y, z, x, y, high, middle, low, 1.0, 1.0, 1.0], 16).T.astype(BF16)


def source_features(off, row_off, col_off):
    x, y, z = off[0:1], off[1:2], off[2:3]
    x_moved, y_moved = x + col_off, y + row_off
    high, middle, low = three_parts(PANELS * (x_moved * x_moved + y_moved * y_moved + z * z))
    twice = -2.0 * PANELS
    return rows_of(
        [twice * x, twice * y, twice * z, twice * col_off, twice * row_off, 1.0, 1.0, 1.0, high, middle, low], 16
    ).astype(BF16)


def near_pairs(pairs, mask, listed, target_feats, source_offs, source_charges, acc):
    count = jnp.int32(0)
    for target, slot, source, row_off, col_off in pairs:
        listed[count] = target + 16 * source + 256 * (row_off + 1) + 1024 * (col_off + 1)
        count = count + (1 if slot is None else mask[target, slot])

    def one(index):
        code = listed[index]
        target = code & 15
        source = (code >> 4) & 15
        row_off = ((code >> 8) & 3) - 1
        col_off = ((code >> 10) & 3) - 1
        moved = source_features(source_offs[source, 0:3, :], row_off.astype(F32), col_off.astype(F32))
        squared = jnp.dot(target_feats[target], moved, preferred_element_type=F32)
        tile = lax.rsqrt(squared).astype(BF16)
        acc[target] += lax.dot_general(source_charges[source], tile, NT, preferred_element_type=F32)

    def several(step, carry):
        for k in range(4):
            one(4 * step + k)
        return carry

    def single(step, carry):
        one(step)
        return carry

    fours = count // 4
    lax.fori_loop(0, fours, several, 0)
    lax.fori_loop(4 * fours, count, single, 0)


def slot_of(row_off, col_off):
    place = 3 * (row_off + 1) + col_off + 1
    return None if place == 4 else place - (place > 4)


def inner_pairs(row):
    found = []
    for col in range(4):
        for row_off in (-1, 0, 1):
            for col_off in (-1, 0, 1):
                at_row, at_col = row + row_off, col + col_off
                if 0 <= at_row < 2 and 0 <= at_col < 4:
                    found.append((4 * row + col, slot_of(row_off, col_off), 4 * at_row + at_col, row_off, col_off))
    return found


def row_pairs():
    found = []
    for row, row_off in ((0, -1), (1, 1)):
        for col in range(4):
            for col_off in (-1, 0, 1):
                if 0 <= col + col_off < 4:
                    found.append((4 * row + col, slot_of(row_off, col_off), 4 * row + col + col_off, row_off, col_off))
    return found


def col_pairs():
    found = []
    for side, col, col_off in ((0, 0, -1), (1, 3, 1)):
        for row in range(2):
            for row_off in (-1, 0, 1):
                found.append((4 * row + col, slot_of(row_off, col_off), 4 * side + row + row_off + 1, row_off, col_off))
    return found


def first_kernel(charges, offsets, basis, transfer, parent, up, down, small, poles_out):
    poles = []
    box = jnp.zeros((RANK, LOADS), F32)
    for leaf in range(8):
        pole = lax.dot_general(basis[leaf], charges[leaf], NT, preferred_element_type=F32).astype(BF16)
        poles.append(pole)
        box = box + lax.dot_general(transfer[leaf], pole, TN, preferred_element_type=F32)
    box = box.astype(BF16)
    small[0] = fold(box)
    for level in range(2):
        term = lax.dot_general(parent[level], box, TN, preferred_element_type=F32)
        small[1 + level] = fold(term.astype(BF16))
    pairs = [jnp.concatenate([poles[2 * k], poles[2 * k + 1]], axis=1) for k in range(4)]
    for k in range(4):
        poles_out[k] = pairs[k]
    for row, buffer in ((0, down), (1, up)):
        offs = []
        for col in range(4):
            leaf = 4 * row + col
            buffer[64 * col : 64 * (col + 1), :] = charges[leaf]
            off = offsets[leaf].astype(F32)
            offs += [off[0:1], off[1:2], off[2:3]]
        buffer[ROW_OFFS:ROW_POLES, :] = rows_of(offs, 16).astype(BF16)
        for k in range(4):
            buffer[ROW_POLES:ROW_BOX, 128 * k : 128 * (k + 1)] = pairs[k]
        buffer[ROW_BOX:ROW_ALL, 0:256] = flat(fold(box))
        buffer[ROW_BOX:ROW_ALL, 256:512] = jnp.zeros((16, 256), BF16)


def inner_kernel(row, mask, charges, offsets, out, listed, feats, offs, acc):
    for leaf in range(8):
        offs[leaf, 0:3, :] = offsets[leaf].astype(F32)
    for col in range(4):
        feats[4 * row + col] = target_features(offs[4 * row + col, 0:3, :])
        acc[4 * row + col] = jnp.zeros((LOADS, PANELS), F32)
    near_pairs(inner_pairs(row), mask, listed, feats, offs, charges, acc)
    out[...] = acc[4 * row : 4 * row + 4]


def spread_offsets(packed, offs, base):
    values = packed.astype(F32)
    for leaf in range(4):
        offs[base + leaf, 0:3, :] = values[3 * leaf : 3 * leaf + 3]


def row_kernel(mask, offsets, top, bottom, out, listed, feats, offs, charges, acc):
    for leaf in range(8):
        feats[leaf] = target_features(offsets[leaf].astype(F32))
    for side, buffer in ((0, top), (1, bottom)):
        spread_offsets(buffer[ROW_OFFS:ROW_POLES, :], offs, 4 * side)
        for col in range(4):
            charges[4 * side + col] = buffer[64 * col : 64 * (col + 1), :]
    acc[...] = jnp.zeros_like(acc)
    near_pairs(row_pairs(), mask, listed, feats, offs, charges, acc)
    out[...] = acc[...]


def pack_kernel(charges, offsets, poles, top, bottom, boxes, right, left):
    for buffer, col in ((right, 3), (left, 0)):
        pair = col // 2
        offs = []
        for place, source in enumerate((top, None, None, bottom)):
            if source is None:
                leaf = 4 * (place - 1) + col
                buffer[64 * place : 64 * (place + 1), :] = charges[leaf]
                off = offsets[leaf].astype(F32)
            else:
                buffer[64 * place : 64 * (place + 1), :] = source[64 * col : 64 * (col + 1), :]
                off = source[ROW_OFFS:ROW_POLES, :].astype(F32)[3 * col : 3 * col + 3]
            offs += [off[0:1], off[1:2], off[2:3]]
        buffer[COL_OFFS:COL_POLES, :] = rows_of(offs, 16).astype(BF16)
        for row in range(6):
            if row < 2:
                start = 128 * (2 * row + pair)
                pole = top[ROW_POLES:ROW_BOX, start : start + 128]
            elif row < 4:
                pole = poles[2 * (row - 2) + pair]
            else:
                start = 128 * (2 * (row - 4) + pair)
                pole = bottom[ROW_POLES:ROW_BOX, start : start + 128]
            base, lane = COL_POLES + 32 * (row // 2), 256 * (row % 2)
            buffer[base : base + 32, lane : lane + 128] = pole[:32]
            buffer[base : base + 32, lane + 128 : lane + 256] = pole[32:]
        for row in range(5):
            base, lane = COL_BOX + 16 * (row // 2), 256 * (row % 2)
            buffer[base : base + 16, lane : lane + 256] = flat(boxes[row])
        buffer[COL_BOX + 32 : COL_ALL, 256:512] = jnp.zeros((16, 256), BF16)


def flag_row(flags, which):
    row = lax.broadcasted_iota(jnp.int32, (32, WIDE), 0)
    lane = lax.broadcasted_iota(jnp.int32, (32, WIDE), 1)
    spread = jnp.where((lane >> 6) == row, 1.0, 0.0).astype(BF16)
    return jnp.dot(flags, spread, preferred_element_type=F32)


def box_product(coupling, flags, window):
    return jnp.dot(coupling * flags, window, preferred_element_type=F32)


def edge_kernel(
    mask, offsets, left, right, inner_top, inner_bottom, by_rows, poles, top, bottom, flags, coupling,
    box_coupling, boxes, far_left, far_right,
    out, leaf_out, box_out, listed, feats, offs, charges, acc, table, window,
):
    for col in (0, 3):
        for row in range(2):
            feats[4 * row + col] = target_features(offsets[4 * row + col].astype(F32))
    for side, buffer in ((0, left), (1, right)):
        spread_offsets(buffer[COL_OFFS:COL_POLES, :], offs, 4 * side)
        for place in range(4):
            charges[4 * side + place] = buffer[64 * place : 64 * (place + 1), :]
    acc[0:4] = inner_top[...] + by_rows[0:4]
    acc[4:8] = inner_bottom[...] + by_rows[4:8]
    near_pairs(col_pairs(), mask, listed, feats, offs, charges, acc)
    out[...] = acc[...]
    for row in range(6):
        for pair in range(4):
            if pair in (0, 3):
                buffer = left if pair == 0 else right
                base, lane = COL_POLES + 32 * (row // 2), 256 * (row % 2)
                both = jnp.concatenate(
                    [buffer[base : base + 32, lane : lane + 128], buffer[base : base + 32, lane + 128 : lane + 256]], axis=0
                )
            elif row in (2, 3):
                both = poles[2 * (row - 2) + pair - 1]
            else:
                buffer, at = (top, row) if row < 2 else (bottom, row - 4)
                start = 128 * (2 * at + pair - 1)
                both = buffer[ROW_POLES:ROW_BOX, start : start + 128]
            table[row, 128 * pair : 128 * pair + 64, :] = both[:, :64]
            table[row, 128 * pair + 64 : 128 * pair + 128, :] = both[:, 64:]
    spread = flag_row(flags[...], 0).astype(BF16)
    for row in range(2):
        for col in range(4):
            leaf = 4 * row + col
            seen = jnp.concatenate([table[row + a, 64 * col : 64 * (col + 5), :] for a in range(5)], axis=0)
            leaf_out[leaf] = box_product(coupling[leaf], spread[leaf : leaf + 1], seen)
    for row in range(5):
        base, lane = COL_BOX + 16 * (row // 2), 256 * (row % 2)
        found = (
            far_left[row],
            unflat(left[base : base + 16, lane : lane + 256]),
            boxes[row],
            unflat(right[base : base + 16, lane : lane + 256]),
            far_right[row],
        )
        for col in range(5):
            start = 64 * (5 * row + col)
            window[start : start + 64, :] = unfold(found[col])
    box_out[...] = box_product(box_coupling[0], spread[8:9], window[...])


def last_kernel(
    near, leaf_local, box_one, flags, box_coupling, transfer, basis,
    box2, box2_left, box2_right, box3, box4_left, box4_right, box8, group,
    out, window,
):
    spread = flag_row(flags[...], 0).astype(BF16)
    total = box_one[...]
    lower = (group[0] < 2).astype(BF16)
    upper = (group[0] >= 2).astype(BF16)
    for level in range(2):
        for row in range(5):
            if level == 0:
                found = (box4_left[row], box2_left[5 + row], box2[row], box2_right[5 + row], box4_right[row])
            else:
                found = (box8[row] * upper, box4_left[5 + row], box3[row], box4_right[5 + row], box8[row] * lower)
            for col in range(5):
                start = 64 * (5 * row + col)
                window[start : start + 64, :] = unfold(found[col])
        total = total + box_product(box_coupling[1 + level], spread[9 + level : 10 + level], window[...])
    total = total.astype(BF16)
    for leaf in range(8):
        local = leaf_local[leaf] + jnp.dot(transfer[leaf], total, preferred_element_type=F32)
        far = lax.dot_general(local.astype(BF16), basis[leaf], TN, preferred_element_type=F32)
        out[leaf] = (near[leaf] + far).astype(BF16)


def near_scratch(sources):
    return [
        pltpu.SMEM((32,), jnp.int32),
        pltpu.VMEM((8, PANELS, 16), BF16),
        pltpu.VMEM((8, 8, PANELS), F32),
        *([pltpu.VMEM((8, LOADS, PANELS), BF16)] if sources else []),
        pltpu.VMEM((8, LOADS, PANELS), F32),
    ]


def body(
    charges,
    offsets,
    leaf_basis,
    near_mask,
    leaf_coupling,
    leaf_distant_flags,
    leaf_transfer,
    box_coupling,
    box_far,
    parent_child_transfer,
):
    charges = charges.reshape(8, LOADS, PANELS)
    offsets = offsets.reshape(8, 3, PANELS)
    basis = leaf_basis.reshape(8, RANK, PANELS)
    mask = near_mask.reshape(8, 8)
    coupling = leaf_coupling.reshape(8, RANK, WIDE)
    transfer = leaf_transfer.reshape(8, RANK, RANK)
    box_coupling = box_coupling.reshape(3, RANK, WIDE)
    parent = parent_child_transfer.reshape(2, RANK, RANK)
    flags = jnp.concatenate([leaf_distant_flags.reshape(8, 25), box_far.reshape(3, 25)], axis=0)
    flags = jnp.pad(flags, ((0, 5), (0, 7))).astype(BF16)
    row_at, col_at = lax.axis_index("row"), lax.axis_index("col")

    up, down, small, poles = kernel_call(
        first_kernel,
        (shape((ROW_ALL, 512)), shape((ROW_ALL, 512)), shape((3, 32, 128)), shape((4, 64, 128))),
        [], "first", 10**9, charges, offsets, basis, transfer, parent,
    )
    terms = small[1:3]
    terms_peer = swapped(terms, "row", 0)
    top = shifted(up, "row", 1)
    bottom = shifted(down, "row", -1)
    near_cost = 6 * 10**9
    inner = [
        kernel_call(
            functools.partial(inner_kernel, row), shape((4, LOADS, PANELS), F32), near_scratch(False),
            f"inner{row}", near_cost, mask, charges, offsets, smem=(0,),
        )
        for row in range(2)
    ]
    sums = terms.astype(F32) + terms_peer.astype(F32)
    sums = sums + swapped(sums.astype(BF16), "col", 0).astype(F32)
    box1, sums = small[0], sums.astype(BF16)
    near_by_two = jnp.concatenate([box1[None], sums], axis=0)
    above = shifted(near_by_two, "row", 2)
    below = shifted(near_by_two, "row", -2)
    second_even = (row_at // 2) % 2 == 0
    row3 = sums[1].astype(F32) + jnp.where(second_even, below[2], above[2]).astype(F32)
    row3 = row3.astype(BF16)
    by_four = jnp.stack([sums[0], row3])
    above4, below4 = shifted(by_four, "row", 4), shifted(by_four, "row", -4)
    above8, below8 = shifted(row3, "row", 8), shifted(row3, "row", -8)

    def box_from(buffer):
        flattened = buffer[ROW_BOX:ROW_ALL, 0:256]
        return jnp.concatenate([flattened[:, :128], flattened[:, 128:]], axis=0)

    boxes1 = jnp.stack([above[0], box_from(top), box1, box_from(bottom), below[0]])
    boxes2 = jnp.stack([above4[0], above[1], sums[0], below[1], below4[0]])
    rows3 = jnp.stack([above8, above4[1], row3, below4[1], below8])
    right, left = kernel_call(
        pack_kernel, (shape((COL_ALL, 512)), shape((COL_ALL, 512))), [], "pack", 10**8,
        charges, offsets, poles, top, bottom, boxes1,
    )
    from_left = shifted(right, "col", 1)
    from_right = shifted(left, "col", -1)
    by_rows = kernel_call(
        row_kernel, shape((8, LOADS, PANELS), F32), near_scratch(True), "byrows", near_cost,
        mask, offsets, top, bottom, smem=(0,),
    )
    stacks = jnp.concatenate([boxes1, boxes2, rows3], axis=0)
    stacks_left = shifted(stacks, "col", 2)
    stacks_right = shifted(stacks, "col", -2)
    second_even = (col_at // 2) % 2 == 0
    boxes3 = rows3.astype(F32) + jnp.where(second_even, stacks_right[10:], stacks_left[10:]).astype(F32)
    boxes3 = boxes3.astype(BF16)
    by_four = jnp.concatenate([boxes2, boxes3], axis=0)
    left4, right4 = shifted(by_four, "col", 4), shifted(by_four, "col", -4)
    across = swapped(boxes3, "col", 3)
    near, leaf_local, box_one = kernel_call(
        edge_kernel,
        (shape((8, LOADS, PANELS), F32), shape((8, RANK, LOADS), F32), shape((RANK, LOADS), F32)),
        near_scratch(True) + [pltpu.VMEM((6, 512, LOADS), BF16), pltpu.VMEM((WIDE, LOADS), BF16)],
        "edge", near_cost, mask, offsets, from_left, from_right, inner[0], inner[1], by_rows, poles, top, bottom,
        flags, coupling, box_coupling, boxes1, stacks_left, stacks_right, smem=(0,),
    )
    group = (col_at // 4).astype(jnp.int32).reshape(1)
    out = kernel_call(
        last_kernel, shape((8, LOADS, PANELS)), [pltpu.VMEM((WIDE, LOADS), BF16)], "last", 10**9,
        near, leaf_local, box_one, flags, box_coupling, transfer, basis,
        boxes2, stacks_left, stacks_right, boxes3, left4, right4, across, group, smem=(14,),
    )
    return out.reshape(2, 4, LOADS, PANELS)


def solution(mesh):
    return jax.shard_map(
        body,
        mesh=mesh,
        in_specs=(
            P("row", "col", None, None),
            P("row", "col", None, None),
            P("row", "col", None, None),
            P("row", "col", None),
            P("row", "col", None, None),
            P("row", "col", None),
            P("row", "col", None, None),
            P("row", "col", None, None, None),
            P("row", "col", None, None),
            P("row", "col", None, None, None),
        ),
        out_specs=P("row", "col", None, None),
        check_vma=False,
    )
```

```python
import functools

import jax
import jax.numpy as jnp
from jax import lax
from jax.experimental import pallas as pl
from jax.experimental.pallas import tpu as pltpu
from jax.sharding import PartitionSpec as P

PANELS = 512
RANK = 64
LOADS = 64
EPSILON = 0.001
F32 = jnp.float32
BF16 = jnp.bfloat16
NT = (((1,), (1,)), ((), ()))
TN = (((0,), (0,)), ((), ()))
WIDE = 25 * RANK
MIB = 2**20
VMEM = pl.BlockSpec(memory_space=pltpu.VMEM)
SMEM = pl.BlockSpec(memory_space=pltpu.SMEM)
HBM = pl.BlockSpec(memory_space=pltpu.HBM)

ROW_OFFS, ROW_POLES, ROW_ALL = 256, 272, 336
COL_OFFS, COL_POLES, COL_BOX, COL_ALL = 256, 272, 368, 416
SUMS = 80


def paired(value, axis, distance):
    return lax.ppermute(value, axis, [(i, i ^ distance) for i in range(lax.axis_size(axis))])


def paired_across(value, axis, distance):
    count = lax.axis_size(axis)
    moves = [(i, i + distance if i & distance else i - distance) for i in range(count)]
    return lax.ppermute(value, axis, [(i, j) for i, j in moves if 0 <= j < count])


def kernel_call(body, outs, scratch, name, cost, *args, smem=(), hbm=(), after=(), limit=40):
    count = len(args)

    def with_order(*refs):
        body(*refs[:count], *refs[count + len(after) :])

    spaces = [SMEM if i in smem else HBM if i in hbm else VMEM for i in range(count)]
    return pl.pallas_call(
        with_order,
        out_shape=outs,
        in_specs=spaces + [VMEM] * len(after),
        out_specs=jax.tree.map(lambda _: VMEM, outs),
        scratch_shapes=scratch,
        compiler_params=pltpu.CompilerParams(vmem_limit_bytes=limit * MIB),
        cost_estimate=pl.CostEstimate(flops=cost, bytes_accessed=4 * MIB, transcendentals=0),
        name=name,
    )(*[pltpu.with_memory_space_constraint(arg, pltpu.HBM) if i in hbm else arg for i, arg in enumerate(args)], *after)


def shape(dims, dtype=BF16):
    return jax.ShapeDtypeStruct(dims, dtype)


def fold(matrix):
    return jnp.concatenate([matrix[:32], matrix[32:]], axis=1)


def unfold(folded):
    return jnp.concatenate([folded[:, :64], folded[:, 64:]], axis=0)


def place_bits():
    row, col = lax.axis_index("row"), lax.axis_index("col")
    return [value & 1 for value in (row, col, row >> 1, row >> 2, row >> 3, col >> 1, col >> 2, col >> 3)]


def flat(folded):
    return jnp.concatenate([folded[:16], folded[16:]], axis=1)


def unflat(flattened):
    return jnp.concatenate([flattened[:, :128], flattened[:, 128:]], axis=0)


def rows_of(values, count):
    row = lax.broadcasted_iota(jnp.int32, (count, PANELS), 0)
    out = jnp.zeros((count, PANELS), F32)
    for index, value in enumerate(values):
        out = jnp.where(row == index, value, out)
    return out


def three_parts(value):
    high = value.astype(BF16).astype(F32)
    rest = value - high
    middle = rest.astype(BF16).astype(F32)
    low = (rest - middle).astype(BF16).astype(F32)
    return high, middle, low


def target_features(off):
    x, y, z = off[0:1], off[1:2], off[2:3]
    high, middle, low = three_parts(PANELS * (x * x + y * y + z * z + EPSILON))
    return rows_of([x, y, z, x, y, high, middle, low, 1.0, 1.0, 1.0], 16).T.astype(BF16)


def source_features(off, row_off, col_off):
    x, y, z = off[0:1], off[1:2], off[2:3]
    x_moved, y_moved = x + col_off, y + row_off
    high, middle, low = three_parts(PANELS * (x_moved * x_moved + y_moved * y_moved + z * z))
    twice = -2.0 * PANELS
    return rows_of(
        [twice * x, twice * y, twice * z, twice * col_off, twice * row_off, 1.0, 1.0, 1.0, high, middle, low], 16
    ).astype(BF16)


def near_pairs(pairs, mask, listed, target_feats, source_offs, source_charges, acc):
    count = jnp.int32(0)
    for target, slot, source, row_off, col_off in pairs:
        listed[count] = target + 16 * source + 256 * (row_off + 1) + 1024 * (col_off + 1)
        count = count + (1 if slot is None else mask[target, slot])

    def one(index):
        code = listed[index]
        target = code & 15
        source = (code >> 4) & 15
        row_off = ((code >> 8) & 3) - 1
        col_off = ((code >> 10) & 3) - 1
        moved = source_features(source_offs[source, 0:3, :], row_off.astype(F32), col_off.astype(F32))
        squared = jnp.dot(target_feats[target], moved, preferred_element_type=F32)
        tile = lax.rsqrt(squared).astype(BF16)
        acc[target] += lax.dot_general(source_charges[source], tile, NT, preferred_element_type=F32)

    def several(step, carry):
        for k in range(4):
            one(4 * step + k)
        return carry

    def single(step, carry):
        one(step)
        return carry

    fours = count // 4
    lax.fori_loop(0, fours, several, 0)
    lax.fori_loop(4 * fours, count, single, 0)


def slot_of(row_off, col_off):
    place = 3 * (row_off + 1) + col_off + 1
    return None if place == 4 else place - (place > 4)


def inner_pairs(targets):
    found = []
    for target in targets:
        row, col = divmod(target, 4)
        for row_off in (-1, 0, 1):
            for col_off in (-1, 0, 1):
                at_row, at_col = row + row_off, col + col_off
                if 0 <= at_row < 2 and 0 <= at_col < 4:
                    found.append((target, slot_of(row_off, col_off), 4 * at_row + at_col, row_off, col_off))
    return found


def row_pairs():
    found = []
    for row, row_off in ((0, -1), (1, 1)):
        for col in range(4):
            for col_off in (-1, 0, 1):
                if 0 <= col + col_off < 4:
                    found.append((4 * row + col, slot_of(row_off, col_off), 4 * row + col + col_off, row_off, col_off))
    return found


def col_pairs():
    found = []
    for side, col, col_off in ((0, 0, -1), (1, 3, 1)):
        for row in range(2):
            for row_off in (-1, 0, 1):
                found.append((4 * row + col, slot_of(row_off, col_off), 4 * side + row + row_off + 1, row_off, col_off))
    return found


def first_kernel(
    charges_hbm, offsets_hbm, basis_hbm, transfer_hbm, parent_hbm,
    with_pair, across, small, poles_out,
    charges, offsets, basis, transfer, parent, sems,
):
    side = place_bits()[0]
    loads = []
    for k in range(4):
        rows = pl.ds(2 * k, 2)
        loads.append(pltpu.make_async_copy(charges_hbm.at[rows], charges.at[rows], sems.at[k]))
        loads.append(pltpu.make_async_copy(basis_hbm.at[rows], basis.at[rows], sems.at[4 + k]))
    loads.append(pltpu.make_async_copy(transfer_hbm, transfer, sems.at[8]))
    loads.append(pltpu.make_async_copy(parent_hbm, parent, sems.at[9]))
    loads.append(pltpu.make_async_copy(offsets_hbm, offsets, sems.at[10]))
    for load in loads:
        load.start()
    loads[10].wait()
    offs = [[offsets[row, k].astype(F32) for k in range(3)] for row in range(2)]
    halves = [rows_of([offs[row][k % 3][k // 3 : k // 3 + 1] for k in range(12)], 16).astype(BF16) for row in range(2)]
    with_pair[ROW_OFFS:ROW_POLES, :] = jnp.where(side == 0, halves[1], halves[0])
    across[ROW_OFFS:ROW_POLES, :] = jnp.where(side == 0, halves[0], halves[1])
    poles = []
    for k in range(4):
        loads[2 * k].wait()
        loads[2 * k + 1].wait()
        for leaf in (2 * k, 2 * k + 1):
            poles.append(lax.dot_general(basis[leaf], charges[leaf], NT, preferred_element_type=F32).astype(BF16))
    loads[8].wait()
    box = jnp.zeros((RANK, LOADS), F32)
    for leaf in range(8):
        box = box + lax.dot_general(transfer[leaf], poles[leaf], TN, preferred_element_type=F32)
    box = box.astype(BF16)
    small[0] = fold(box)
    loads[9].wait()
    for level in range(2):
        term = lax.dot_general(parent[level], box, TN, preferred_element_type=F32)
        small[1 + level] = fold(term.astype(BF16))
    pairs = [jnp.concatenate([poles[2 * k], poles[2 * k + 1]], axis=1) for k in range(4)]
    for k in range(4):
        poles_out[k] = pairs[k]
    for buffer, row in ((with_pair, 1 - side), (across, side)):
        for col in range(4):
            buffer[64 * col : 64 * (col + 1), :] = charges[4 * row + col]
        for k in range(4):
            buffer[ROW_POLES:ROW_ALL, 128 * k : 128 * (k + 1)] = pairs[k]


def own_offsets(offsets, offs):
    for row in range(2):
        for k in range(3):
            values = offsets[row, k].astype(F32)
            for col in range(4):
                offs[4 * row + col, k : k + 1, :] = values[col : col + 1]


def inner_kernel(targets, mask, charges, offsets, out, listed, feats, offs, acc):
    own_offsets(offsets, offs)
    for target in targets:
        feats[target] = target_features(offs[target, 0:3, :])
        acc[target] = jnp.zeros((LOADS, PANELS), F32)
    near_pairs(inner_pairs(targets), mask, listed, feats, offs, charges, acc)
    out[...] = acc[targets[0] : targets[-1] + 1]


def spread_offsets(packed, offs, base):
    values = packed.astype(F32)
    for leaf in range(4):
        offs[base + leaf, 0:3, :] = values[3 * leaf : 3 * leaf + 3]


def row_kernel(mask, offsets, paired_rows, across_rows, out, listed, feats, offs, charges, acc):
    place = place_bits()
    own_offsets(offsets, offs)
    for leaf in range(8):
        feats[leaf] = target_features(offs[leaf, 0:3, :])
    for side, buffer in ((1 - place[0], paired_rows), (place[0], across_rows)):
        spread_offsets(buffer[ROW_OFFS:ROW_POLES, :], offs, 4 * side)
        for col in range(4):
            charges[4 * side + col] = buffer[64 * col : 64 * (col + 1), :]
    acc[...] = jnp.zeros_like(acc)
    near_pairs(row_pairs(), mask, listed, feats, offs, charges, acc)
    out[...] = acc[...]


def pack_kernel(
    charges, offsets, poles, paired_rows, across_rows, small, pair1, pair2, pair4, pair8, across8,
    with_pair, across, boxes_out, sums_out,
):
    place = place_bits()
    bit0, bit1, bit2 = place[0], place[2], place[3]
    at = bit0 == 0
    minus8, plus8 = [[jnp.where(place[4] == want, pair8[k], across8[k]) for k in range(6)] for want in (1, 0)]
    low2, low4 = bit1 == 0, bit2 == 0
    minus2, plus2 = [], []
    for k in range(3):
        other = jnp.where(low2 != low4, pair4[2 + k], jnp.where(low2, minus8[3 + k], plus8[3 + k]))
        minus2.append(jnp.where(low2, other, pair2[k]))
        plus2.append(jnp.where(low2, pair2[k], other))
    boxes = [
        minus2[0],
        jnp.where(at, minus2[1], pair1[0]),
        small[0],
        jnp.where(at, pair1[0], plus2[1]),
        plus2[0],
    ]
    own2 = (small[1].astype(F32) + pair1[1].astype(F32)).astype(BF16)
    own3 = (small[2].astype(F32) + pair1[2].astype(F32) + pair2[3].astype(F32)).astype(BF16)
    second = [
        jnp.where(low4, minus8[2], pair4[0]),
        minus2[2],
        own2,
        plus2[2],
        jnp.where(low4, pair4[0], plus8[2]),
    ]
    third = [
        minus8[0],
        jnp.where(low4, minus8[1], pair4[1]),
        own3,
        jnp.where(low4, pair4[1], plus8[1]),
        plus8[0],
    ]
    for row in range(5):
        base, lane = 16 * (row // 2), 256 * (row % 2)
        piece = flat(boxes[row])
        boxes_out[base : base + 16, lane : lane + 256] = piece
        for buffer in (with_pair, across):
            buffer[COL_BOX + base : COL_BOX + base + 16, lane : lane + 256] = piece
        for half, found in enumerate((second, third)):
            piece = flat(found[row])
            sums_out[16 * row : 16 * row + 16, 256 * half : 256 * half + 256] = piece
            with_pair[COL_ALL + 16 * row : COL_ALL + 16 * row + 16, 256 * half : 256 * half + 256] = piece
    blank = jnp.zeros((16, 256), BF16)
    boxes_out[32:48, 256:512] = blank
    for buffer in (with_pair, across):
        buffer[COL_BOX + 32 : COL_ALL, 256:512] = blank

    def fill(buffer, col, top, bottom):
        pair = col // 2
        offs = []
        for spot, source in enumerate((top, None, None, bottom)):
            if source is None:
                leaf = 4 * (spot - 1) + col
                buffer[64 * spot : 64 * (spot + 1), :] = charges[leaf]
                offs += [offsets[spot - 1, k].astype(F32)[col : col + 1] for k in range(3)]
            else:
                buffer[64 * spot : 64 * (spot + 1), :] = source[64 * col : 64 * (col + 1), :]
                off = source[ROW_OFFS:ROW_POLES, :].astype(F32)[3 * col : 3 * col + 3]
                offs += [off[0:1], off[1:2], off[2:3]]
        buffer[COL_OFFS:COL_POLES, :] = rows_of(offs, 16).astype(BF16)
        for row in range(6):
            if row in (2, 3):
                pole = poles[2 * (row - 2) + pair]
            else:
                source = top if row < 2 else bottom
                start = 128 * (2 * (row % 4) + pair)
                pole = source[ROW_POLES:ROW_ALL, start : start + 128]
            base, lane = COL_POLES + 32 * (row // 2), 256 * (row % 2)
            buffer[base : base + 32, lane : lane + 128] = pole[:32]
            buffer[base : base + 32, lane + 128 : lane + 256] = pole[32:]

    for row_side in range(2):
        for col_side in range(2):

            @pl.when((place[0] == row_side) & (place[1] == col_side))
            def _():
                top, bottom = (across_rows, paired_rows) if row_side == 0 else (paired_rows, across_rows)
                fill(with_pair, 0 if col_side else 3, top, bottom)
                fill(across, 3 if col_side else 0, top, bottom)


def flag_row(flags):
    row = lax.broadcasted_iota(jnp.int32, (32, WIDE), 0)
    lane = lax.broadcasted_iota(jnp.int32, (32, WIDE), 1)
    spread = jnp.where((lane >> 6) == row, 1.0, 0.0).astype(BF16)
    return jnp.dot(flags, spread, preferred_element_type=F32).astype(BF16)


def box_product(coupling, flags, window):
    return jnp.dot(coupling * flags, window, preferred_element_type=F32)


def edge_kernel(
    mask, offsets, paired_cols, across_cols, inner0, inner1, by_rows, poles, paired_rows, across_rows, flags, coupling,
    out, leaf_out, listed, feats, offs, charges, acc, table,
):
    place = place_bits()
    own_offsets(offsets, offs)
    for leaf in (0, 3, 4, 7):
        feats[leaf] = target_features(offs[leaf, 0:3, :])
    for side, buffer in ((1 - place[1], paired_cols), (place[1], across_cols)):
        spread_offsets(buffer[COL_OFFS:COL_POLES, :], offs, 4 * side)
        for spot in range(4):
            charges[4 * side + spot] = buffer[64 * spot : 64 * (spot + 1), :]
    acc[0:3] = inner0[...] + by_rows[0:3]
    acc[3:6] = inner1[...] + by_rows[3:6]
    acc[6:8] = by_rows[6:8]
    near_pairs(col_pairs(), mask, listed, feats, offs, charges, acc)
    out[...] = acc[...]

    def put(row, pair, both):
        table[row, 128 * pair : 128 * pair + 64, :] = both[:, :64]
        table[row, 128 * pair + 64 : 128 * pair + 128, :] = both[:, 64:]

    for row in (2, 3):
        for pair in (1, 2):
            put(row, pair, poles[2 * (row - 2) + pair - 1])
    for side in range(2):

        @pl.when(place[0] == side)
        def _():
            for base, buffer in ((4 - 4 * side, paired_rows), (4 * side, across_rows)):
                for row in range(2):
                    for pair in (1, 2):
                        start = 128 * (2 * row + pair - 1)
                        put(base + row, pair, buffer[ROW_POLES:ROW_ALL, start : start + 128])

        @pl.when(place[1] == side)
        def _():
            for pair, buffer in ((3 - 3 * side, paired_cols), (3 * side, across_cols)):
                for row in range(6):
                    base, lane = COL_POLES + 32 * (row // 2), 256 * (row % 2)
                    put(row, pair, unflat(buffer[base : base + 32, lane : lane + 256]))

    spread = flag_row(flags[...])
    for row in range(2):
        for col in range(4):
            leaf = 4 * row + col
            seen = jnp.concatenate([table[row + a, 64 * col : 64 * (col + 5), :] for a in range(5)], axis=0)
            leaf_out[leaf] = box_product(coupling[leaf], spread[leaf : leaf + 1], seen)


def inner_box_kernel(
    targets, mask, charges, offsets, flags, box_coupling, boxes, paired_cols, across_cols, pair2, across2,
    out, box_out, listed, feats, offs, acc, window,
):
    inner_kernel(targets, mask, charges, offsets, out, listed, feats, offs, acc)
    place = place_bits()
    low1, low2 = place[1] == 0, place[5] == 0
    for row in range(5):
        base, lane = 16 * (row // 2), 256 * (row % 2)
        pair_1 = paired_cols[COL_BOX + base : COL_BOX + base + 16, lane : lane + 256]
        across_1 = across_cols[COL_BOX + base : COL_BOX + base + 16, lane : lane + 256]
        pair_2, across_2 = [ref[base : base + 16, lane : lane + 256] for ref in (pair2, across2)]
        found = (
            jnp.where(low2, across_2, pair_2),
            jnp.where(low1, across_1, pair_1),
            boxes[base : base + 16, lane : lane + 256],
            jnp.where(low1, pair_1, across_1),
            jnp.where(low2, pair_2, across_2),
        )
        for col in range(5):
            start = 64 * (5 * row + col)
            window[start : start + 64, :] = unfold(unflat(found[col]))
    box_out[...] = box_product(box_coupling[0], flag_row(flags[...])[8:9], window[...])


def last_kernel(
    near, inner2, leaf_local, box_one, flags, box_coupling, transfer, basis,
    sums, pair2, across2, boxes3, pair4, across4, pair8,
    out, window,
):
    place = place_bits()
    spread = flag_row(flags[...])
    total = box_one[...]
    low2, low4, low8 = place[5] == 0, place[6] == 0, place[7] == 0
    blank = jnp.zeros((16, 256), BF16)
    for level in range(2):
        lanes = slice(256 * level, 256 * level + 256)
        for row in range(5):
            rows = slice(16 * row, 16 * row + 16)
            later = slice(48 + 16 * row, 64 + 16 * row)
            pair_4, across_4 = pair4[rows, lanes], across4[rows, lanes]
            minus4, plus4 = jnp.where(low4, across_4, pair_4), jnp.where(low4, pair_4, across_4)
            if level == 0:
                pair_2, across_2 = pair2[later, lanes], across2[later, lanes]
                minus2, plus2 = jnp.where(low2, across_2, pair_2), jnp.where(low2, pair_2, across_2)
                found = (minus4, minus2, sums[rows, lanes], plus2, plus4)
            else:
                far = pair8[rows, :]
                found = (jnp.where(low8, blank, far), minus4, boxes3[rows, :], plus4, jnp.where(low8, far, blank))
            for col in range(5):
                start = 64 * (5 * row + col)
                window[start : start + 64, :] = unfold(unflat(found[col]))
        total = total + box_product(box_coupling[1 + level], spread[9 + level : 10 + level], window[...])
    total = total.astype(BF16)
    for leaf in range(8):
        local = leaf_local[leaf] + jnp.dot(transfer[leaf], total, preferred_element_type=F32)
        far = lax.dot_general(local.astype(BF16), basis[leaf], TN, preferred_element_type=F32)
        direct = near[leaf] + inner2[leaf - 6] if leaf >= 6 else near[leaf]
        out[leaf] = (direct + far).astype(BF16)


def near_scratch(sources):
    return [
        pltpu.SMEM((32,), jnp.int32),
        pltpu.VMEM((8, PANELS, 16), BF16),
        pltpu.VMEM((8, 8, PANELS), F32),
        *([pltpu.VMEM((8, LOADS, PANELS), BF16)] if sources else []),
        pltpu.VMEM((8, LOADS, PANELS), F32),
    ]


def body(
    charges,
    offsets,
    leaf_basis,
    near_mask,
    leaf_coupling,
    leaf_distant_flags,
    leaf_transfer,
    box_coupling,
    box_far,
    parent_child_transfer,
):
    charges = charges.reshape(8, LOADS, PANELS)
    offsets = offsets.transpose(0, 2, 1, 3)
    basis = leaf_basis.reshape(8, RANK, PANELS)
    mask = near_mask.reshape(8, 8)
    coupling = leaf_coupling.reshape(8, RANK, WIDE)
    transfer = leaf_transfer.reshape(8, RANK, RANK)
    box_coupling = box_coupling.reshape(3, RANK, WIDE)
    parent = parent_child_transfer.reshape(2, RANK, RANK)
    flags = jnp.concatenate([leaf_distant_flags.reshape(8, 25), box_far.reshape(3, 25)], axis=0)
    flags = jnp.pad(flags, ((0, 5), (0, 7))).astype(BF16)
    near_cost = 6 * 10**9
    rows_pair, rows_across, small, poles = kernel_call(
        first_kernel,
        (shape((ROW_ALL, 512)), shape((ROW_ALL, 512)), shape((3, 32, 128)), shape((4, 64, 128))),
        [
            pltpu.VMEM((8, LOADS, PANELS), BF16),
            pltpu.VMEM((2, 3, 4, PANELS), BF16),
            pltpu.VMEM((8, RANK, PANELS), BF16),
            pltpu.VMEM((8, RANK, RANK), BF16),
            pltpu.VMEM((2, RANK, RANK), BF16),
            pltpu.SemaphoreType.DMA((11,)),
        ],
        "first", 10**9, charges, offsets, basis, transfer, parent, hbm=(0, 1, 2, 3, 4),
    )

    pair1 = paired(small, "row", 1)
    paired_rows = paired(rows_pair, "row", 1)
    across_rows = paired_across(rows_across, "row", 1)
    halves = (small[1:3].astype(F32) + pair1[1:3].astype(F32)).astype(BF16)
    payload = jnp.concatenate([small[:1], pair1[:1], halves], axis=0)
    pair2 = paired(payload, "row", 2)
    inner0 = kernel_call(
        functools.partial(inner_kernel, (0, 1, 2)), shape((3, LOADS, PANELS), F32), near_scratch(False), "inner0",
        near_cost, mask, charges, offsets, smem=(0,), after=(payload,),
    )
    pair2, inner0 = lax.optimization_barrier((pair2, inner0))
    quarter = (small[2].astype(F32) + pair1[2].astype(F32) + pair2[3].astype(F32)).astype(BF16)
    payload = jnp.concatenate([halves[:1], quarter[None], pair2[:3]], axis=0)
    pair4 = paired(payload, "row", 4)
    inner1 = kernel_call(
        functools.partial(inner_kernel, (3, 4, 5)), shape((3, LOADS, PANELS), F32), near_scratch(False), "inner1",
        near_cost, mask, charges, offsets, smem=(0,), after=(payload,),
    )
    pair4, inner1 = lax.optimization_barrier((pair4, inner1))
    payload = jnp.concatenate([quarter[None], pair4[1:2], pair4[0:1], pair4[2:5]], axis=0)
    pair8, across8 = paired(payload, "row", 8), paired_across(payload, "row", 8)
    by_rows = kernel_call(
        row_kernel, shape((8, LOADS, PANELS), F32), near_scratch(True), "byrows", near_cost,
        mask, offsets, paired_rows, across_rows, smem=(0,), after=(payload,),
    )

    pair8, across8, by_rows = lax.optimization_barrier((pair8, across8, by_rows))

    cols_pair, cols_across, boxes1, row_sums = kernel_call(
        pack_kernel,
        (shape((COL_ALL + SUMS, 512)), shape((COL_ALL, 512)), shape((48, 512)), shape((SUMS, 512))),
        [], "pack", 10**8, charges, offsets, poles, paired_rows, across_rows,
        small, pair1, pair2, pair4, pair8, across8,
    )
    paired_cols = paired(cols_pair, "col", 1)
    across_cols = paired_across(cols_across, "col", 1)
    sums = (row_sums.astype(F32) + paired_cols[COL_ALL:].astype(F32)).astype(BF16)
    payload = jnp.concatenate([boxes1, sums], axis=0)
    col_pair2, col_across2 = paired(payload, "col", 2), paired_across(payload, "col", 2)
    near, leaf_local = kernel_call(
        edge_kernel,
        (shape((8, LOADS, PANELS), F32), shape((8, RANK, LOADS), F32)),
        near_scratch(True) + [pltpu.VMEM((6, 512, LOADS), BF16)], "edge", near_cost,
        mask, offsets, paired_cols, across_cols, inner0, inner1, by_rows, poles, paired_rows, across_rows,
        flags, coupling, smem=(0,), after=(payload,),
    )
    boxes3 = (sums[:, 256:].astype(F32) + col_pair2[48:, 256:].astype(F32)).astype(BF16)
    payload = jnp.concatenate([sums[:, :256], boxes3], axis=1)
    col_pair4, col_across4 = paired(payload, "col", 4), paired_across(payload, "col", 4)
    col_pair8 = paired(boxes3, "col", 8)
    inner2, box_one = kernel_call(
        functools.partial(inner_box_kernel, (6, 7)),
        (shape((2, LOADS, PANELS), F32), shape((RANK, LOADS), F32)),
        near_scratch(False) + [pltpu.VMEM((WIDE, LOADS), BF16)], "inner2", near_cost,
        mask, charges, offsets, flags, box_coupling, boxes1, paired_cols, across_cols, col_pair2, col_across2,
        smem=(0,), after=(payload,),
    )
    out = kernel_call(
        last_kernel, shape((8, LOADS, PANELS)), [pltpu.VMEM((WIDE, LOADS), BF16)], "last", 10**9,
        near, inner2, leaf_local, box_one, flags, box_coupling, transfer, basis,
        sums, col_pair2, col_across2, boxes3, col_pair4, col_across4, col_pair8,
    )
    return out.reshape(2, 4, LOADS, PANELS)


def solution(mesh):
    return jax.shard_map(
        body,
        mesh=mesh,
        in_specs=(
            P("row", "col", None, None),
            P("row", "col", None, None),
            P("row", "col", None, None),
            P("row", "col", None),
            P("row", "col", None, None),
            P("row", "col", None),
            P("row", "col", None, None),
            P("row", "col", None, None, None),
            P("row", "col", None, None),
            P("row", "col", None, None, None),
        ),
        out_specs=P("row", "col", None, None),
        check_vma=False,
    )
```

```python
import functools

import jax
import jax.numpy as jnp
from jax import lax
from jax.experimental import pallas as pl
from jax.experimental.pallas import tpu as pltpu
from jax.sharding import PartitionSpec as P

PANELS = 512
RANK = 64
LOADS = 64
EPSILON = 0.001
F32 = jnp.float32
BF16 = jnp.bfloat16
NT = (((1,), (1,)), ((), ()))
TN = (((0,), (0,)), ((), ()))
WIDE = 25 * RANK
MIB = 2**20
AT_ONCE = (8, 4, 2, 1)
VMEM = pl.BlockSpec(memory_space=pltpu.VMEM)
SMEM = pl.BlockSpec(memory_space=pltpu.SMEM)
HBM = pl.BlockSpec(memory_space=pltpu.HBM)

ROW_OFFS, ROW_POLES, ROW_ALL = 256, 272, 336
COL_OFFS, COL_POLES, COL_BOX, COL_ALL = 256, 272, 368, 416
SUMS = 80


def paired(value, axis, distance):
    return lax.ppermute(value, axis, [(i, i ^ distance) for i in range(lax.axis_size(axis))])


def paired_across(value, axis, distance):
    count = lax.axis_size(axis)
    moves = [(i, i + distance if i & distance else i - distance) for i in range(count)]
    return lax.ppermute(value, axis, [(i, j) for i, j in moves if 0 <= j < count])


def kernel_call(body, outs, scratch, name, cost, *args, smem=(), hbm=(), after=(), out_space=VMEM):
    count = len(args)

    def with_order(*refs):
        body(*refs[:count], *refs[count + len(after) :])

    spaces = [SMEM if i in smem else HBM if i in hbm else VMEM for i in range(count)]
    return pl.pallas_call(
        with_order,
        out_shape=outs,
        in_specs=spaces + [VMEM] * len(after),
        out_specs=jax.tree.map(lambda _: out_space, outs),
        scratch_shapes=scratch,
        compiler_params=pltpu.CompilerParams(vmem_limit_bytes=40 * MIB),
        cost_estimate=pl.CostEstimate(flops=cost, bytes_accessed=4 * MIB, transcendentals=0),
        name=name,
    )(*[pltpu.with_memory_space_constraint(arg, pltpu.HBM) if i in hbm else arg for i, arg in enumerate(args)], *after)


def shape(dims, dtype=BF16):
    return jax.ShapeDtypeStruct(dims, dtype)


def fold(matrix):
    return jnp.concatenate([matrix[:32], matrix[32:]], axis=1)


def unfold(folded):
    return jnp.concatenate([folded[:, :64], folded[:, 64:]], axis=0)


def place_bits():
    row, col = lax.axis_index("row"), lax.axis_index("col")
    return [value & 1 for value in (row, col, row >> 1, row >> 2, row >> 3, col >> 1, col >> 2, col >> 3)]


def flat(folded):
    return jnp.concatenate([folded[:16], folded[16:]], axis=1)


def unflat(flattened):
    return jnp.concatenate([flattened[:, :128], flattened[:, 128:]], axis=0)


def rows_of(values, count):
    row = lax.broadcasted_iota(jnp.int32, (count, PANELS), 0)
    out = jnp.zeros((count, PANELS), F32)
    for index, value in enumerate(values):
        out = jnp.where(row == index, value, out)
    return out


def three_parts(value):
    high = value.astype(BF16).astype(F32)
    rest = value - high
    middle = rest.astype(BF16).astype(F32)
    low = (rest - middle).astype(BF16).astype(F32)
    return high, middle, low


def target_features(off):
    x, y, z = off
    high, middle, low = three_parts(PANELS * (x * x + y * y + z * z + EPSILON))
    return rows_of([x, y, z, x, y, high, middle, low, 1.0, 1.0, 1.0], 16).T.astype(BF16)


def source_features(off, row_off, col_off):
    x, y, z = off[0:1], off[1:2], off[2:3]
    x_moved, y_moved = x + col_off, y + row_off
    high, middle, low = three_parts(PANELS * (x_moved * x_moved + y_moved * y_moved + z * z))
    twice = -2.0 * PANELS
    return rows_of(
        [twice * x, twice * y, twice * z, twice * col_off, twice * row_off, 1.0, 1.0, 1.0, high, middle, low], 16
    ).astype(BF16)


def near_pairs(pairs, mask, listed, target_feats, source_offs, source_charges, acc):
    count = jnp.int32(0)
    for target, slot, source, row_off, col_off in pairs:
        listed[count] = target + 16 * source + 256 * (row_off + 1) + 1024 * (col_off + 1)
        count = count + (1 if slot is None else mask[target, slot])

    def one(index):
        code = listed[index]
        target = code & 15
        source = (code >> 4) & 15
        row_off = ((code >> 8) & 3) - 1
        col_off = ((code >> 10) & 3) - 1
        moved = source_features(source_offs[source, 0:3, :], row_off.astype(F32), col_off.astype(F32))
        squared = jnp.dot(target_feats[target], moved, preferred_element_type=F32)
        tile = lax.rsqrt(squared).astype(BF16)
        acc[target] += lax.dot_general(source_charges[source], tile, NT, preferred_element_type=F32)

    done = jnp.int32(0)
    for at_once in AT_ONCE:
        steps = (count - done) // at_once

        def several(step, carry, done=done, at_once=at_once):
            for k in range(at_once):
                one(done + step * at_once + k)
            return carry

        lax.fori_loop(0, steps, several, 0)
        done = done + steps * at_once


def slot_of(row_off, col_off):
    place = 3 * (row_off + 1) + col_off + 1
    return None if place == 4 else place - (place > 4)


def inner_pairs(targets):
    found = []
    for target in targets:
        row, col = divmod(target, 4)
        for row_off in (-1, 0, 1):
            for col_off in (-1, 0, 1):
                at_row, at_col = row + row_off, col + col_off
                if 0 <= at_row < 2 and 0 <= at_col < 4:
                    found.append((target, slot_of(row_off, col_off), 4 * at_row + at_col, row_off, col_off))
    return found


def row_pairs():
    found = []
    for row, row_off in ((0, -1), (1, 1)):
        for col in range(4):
            for col_off in (-1, 0, 1):
                if 0 <= col + col_off < 4:
                    found.append((4 * row + col, slot_of(row_off, col_off), 4 * row + col + col_off, row_off, col_off))
    return found


def col_pairs():
    found = []
    for side, col, col_off in ((0, 0, -1), (1, 3, 1)):
        for row in range(2):
            for row_off in (-1, 0, 1):
                found.append((4 * row + col, slot_of(row_off, col_off), 4 * side + row + row_off + 1, row_off, col_off))
    return found


def first_kernel(
    charges_hbm, offsets_hbm, basis_hbm, transfer_hbm, parent_hbm,
    with_pair, across, small, poles_out, feats,
    charges, offsets, basis, transfer, parent, sems,
):
    side = place_bits()[0]
    loads = []
    for k in range(4):
        rows = pl.ds(2 * k, 2)
        loads.append(pltpu.make_async_copy(charges_hbm.at[rows], charges.at[rows], sems.at[k]))
        loads.append(pltpu.make_async_copy(basis_hbm.at[rows], basis.at[rows], sems.at[4 + k]))
    loads.append(pltpu.make_async_copy(transfer_hbm, transfer, sems.at[8]))
    loads.append(pltpu.make_async_copy(parent_hbm, parent, sems.at[9]))
    loads.append(pltpu.make_async_copy(offsets_hbm, offsets, sems.at[10]))
    for load in loads:
        load.start()
    loads[10].wait()
    offs = [[offsets[row, k].astype(F32) for k in range(3)] for row in range(2)]
    halves = [rows_of([offs[row][k % 3][k // 3 : k // 3 + 1] for k in range(12)], 16).astype(BF16) for row in range(2)]
    with_pair[ROW_OFFS:ROW_POLES, :] = jnp.where(side == 0, halves[1], halves[0])
    across[ROW_OFFS:ROW_POLES, :] = jnp.where(side == 0, halves[0], halves[1])
    for leaf in range(8):
        row, col = divmod(leaf, 4)
        feats[leaf] = target_features([offs[row][k][col : col + 1] for k in range(3)])
    poles = []
    for k in range(4):
        loads[2 * k].wait()
        loads[2 * k + 1].wait()
        for leaf in (2 * k, 2 * k + 1):
            poles.append(lax.dot_general(basis[leaf], charges[leaf], NT, preferred_element_type=F32).astype(BF16))
    loads[8].wait()
    box = jnp.zeros((RANK, LOADS), F32)
    for leaf in range(8):
        box = box + lax.dot_general(transfer[leaf], poles[leaf], TN, preferred_element_type=F32)
    box = box.astype(BF16)
    small[0] = fold(box)
    loads[9].wait()
    for level in range(2):
        term = lax.dot_general(parent[level], box, TN, preferred_element_type=F32)
        small[1 + level] = fold(term.astype(BF16))
    pairs = [jnp.concatenate([poles[2 * k], poles[2 * k + 1]], axis=1) for k in range(4)]
    for k in range(4):
        poles_out[k] = pairs[k]
    for buffer, row in ((with_pair, 1 - side), (across, side)):
        for col in range(4):
            buffer[64 * col : 64 * (col + 1), :] = charges[4 * row + col]
        for k in range(4):
            buffer[ROW_POLES:ROW_ALL, 128 * k : 128 * (k + 1)] = pairs[k]


def own_offsets(offsets, offs):
    for row in range(2):
        for k in range(3):
            values = offsets[row, k].astype(F32)
            for col in range(4):
                offs[4 * row + col, k : k + 1, :] = values[col : col + 1]


def inner_kernel(targets, mask, charges, offsets, feats, out, listed, offs, acc):
    own_offsets(offsets, offs)
    for target in targets:
        acc[target] = jnp.zeros((LOADS, PANELS), F32)
    near_pairs(inner_pairs(targets), mask, listed, feats, offs, charges, acc)
    out[...] = acc[targets[0] : targets[-1] + 1]


def spread_offsets(packed, offs, base):
    values = packed.astype(F32)
    for leaf in range(4):
        offs[base + leaf, 0:3, :] = values[3 * leaf : 3 * leaf + 3]


def row_kernel(mask, feats, paired_rows, across_rows, out, listed, offs, charges, acc):
    place = place_bits()
    for side, buffer in ((1 - place[0], paired_rows), (place[0], across_rows)):
        spread_offsets(buffer[ROW_OFFS:ROW_POLES, :], offs, 4 * side)
        for col in range(4):
            charges[4 * side + col] = buffer[64 * col : 64 * (col + 1), :]
    acc[...] = jnp.zeros_like(acc)
    near_pairs(row_pairs(), mask, listed, feats, offs, charges, acc)
    out[...] = acc[...]


def pack_kernel(
    charges, offsets, poles, paired_rows, across_rows, small, pair1, pair2, pair4, pair8, across8,
    with_pair, across, boxes_out, sums_out,
):
    place = place_bits()
    bit0, bit1, bit2 = place[0], place[2], place[3]
    at = bit0 == 0
    minus8, plus8 = [[jnp.where(place[4] == want, pair8[k], across8[k]) for k in range(6)] for want in (1, 0)]
    low2, low4 = bit1 == 0, bit2 == 0
    minus2, plus2 = [], []
    for k in range(3):
        other = jnp.where(low2 != low4, pair4[2 + k], jnp.where(low2, minus8[3 + k], plus8[3 + k]))
        minus2.append(jnp.where(low2, other, pair2[k]))
        plus2.append(jnp.where(low2, pair2[k], other))
    boxes = [
        minus2[0],
        jnp.where(at, minus2[1], pair1[0]),
        small[0],
        jnp.where(at, pair1[0], plus2[1]),
        plus2[0],
    ]
    own2 = (small[1].astype(F32) + pair1[1].astype(F32)).astype(BF16)
    own3 = (small[2].astype(F32) + pair1[2].astype(F32) + pair2[3].astype(F32)).astype(BF16)
    second = [
        jnp.where(low4, minus8[2], pair4[0]),
        minus2[2],
        own2,
        plus2[2],
        jnp.where(low4, pair4[0], plus8[2]),
    ]
    third = [
        minus8[0],
        jnp.where(low4, minus8[1], pair4[1]),
        own3,
        jnp.where(low4, pair4[1], plus8[1]),
        plus8[0],
    ]
    for row in range(5):
        base, lane = 16 * (row // 2), 256 * (row % 2)
        piece = flat(boxes[row])
        boxes_out[base : base + 16, lane : lane + 256] = piece
        for buffer in (with_pair, across):
            buffer[COL_BOX + base : COL_BOX + base + 16, lane : lane + 256] = piece
        for half, found in enumerate((second, third)):
            piece = flat(found[row])
            sums_out[16 * row : 16 * row + 16, 256 * half : 256 * half + 256] = piece
            with_pair[COL_ALL + 16 * row : COL_ALL + 16 * row + 16, 256 * half : 256 * half + 256] = piece
    blank = jnp.zeros((16, 256), BF16)
    boxes_out[32:48, 256:512] = blank
    for buffer in (with_pair, across):
        buffer[COL_BOX + 32 : COL_ALL, 256:512] = blank

    def fill(buffer, col, top, bottom):
        pair = col // 2
        offs = []
        for spot, source in enumerate((top, None, None, bottom)):
            if source is None:
                leaf = 4 * (spot - 1) + col
                buffer[64 * spot : 64 * (spot + 1), :] = charges[leaf]
                offs += [offsets[spot - 1, k].astype(F32)[col : col + 1] for k in range(3)]
            else:
                buffer[64 * spot : 64 * (spot + 1), :] = source[64 * col : 64 * (col + 1), :]
                off = source[ROW_OFFS:ROW_POLES, :].astype(F32)[3 * col : 3 * col + 3]
                offs += [off[0:1], off[1:2], off[2:3]]
        buffer[COL_OFFS:COL_POLES, :] = rows_of(offs, 16).astype(BF16)
        for row in range(6):
            if row in (2, 3):
                pole = poles[2 * (row - 2) + pair]
            else:
                source = top if row < 2 else bottom
                start = 128 * (2 * (row % 4) + pair)
                pole = source[ROW_POLES:ROW_ALL, start : start + 128]
            base, lane = COL_POLES + 32 * (row // 2), 256 * (row % 2)
            buffer[base : base + 32, lane : lane + 128] = pole[:32]
            buffer[base : base + 32, lane + 128 : lane + 256] = pole[32:]

    for row_side in range(2):
        for col_side in range(2):

            @pl.when((place[0] == row_side) & (place[1] == col_side))
            def _():
                top, bottom = (across_rows, paired_rows) if row_side == 0 else (paired_rows, across_rows)
                fill(with_pair, 0 if col_side else 3, top, bottom)
                fill(across, 3 if col_side else 0, top, bottom)


def flag_row(flags):
    row = lax.broadcasted_iota(jnp.int32, (32, WIDE), 0)
    lane = lax.broadcasted_iota(jnp.int32, (32, WIDE), 1)
    spread = jnp.where((lane >> 6) == row, 1.0, 0.0).astype(BF16)
    return jnp.dot(flags, spread, preferred_element_type=F32).astype(BF16)


def box_product(coupling, flags, window):
    return jnp.dot(coupling * flags, window, preferred_element_type=F32)


def edge_kernel(
    mask, feats, paired_cols, across_cols, inner0, inner1, inner2, by_rows, poles, paired_rows, across_rows, flags, coupling,
    box_coupling, boxes, pair2, across2, transfer, basis,
    out, box_out, moved_basis, listed, offs, charges, acc, table, window, local,
):
    place = place_bits()
    for side, buffer in ((1 - place[1], paired_cols), (place[1], across_cols)):
        spread_offsets(buffer[COL_OFFS:COL_POLES, :], offs, 4 * side)
        for spot in range(4):
            charges[4 * side + spot] = buffer[64 * spot : 64 * (spot + 1), :]
    acc[0:3] = inner0[...] + by_rows[0:3]
    acc[3:6] = inner1[...] + by_rows[3:6]
    acc[6:8] = inner2[...] + by_rows[6:8]
    near_pairs(col_pairs(), mask, listed, feats, offs, charges, acc)

    def put(row, pair, both):
        table[row, 128 * pair : 128 * pair + 64, :] = both[:, :64]
        table[row, 128 * pair + 64 : 128 * pair + 128, :] = both[:, 64:]

    for row in (2, 3):
        for pair in (1, 2):
            put(row, pair, poles[2 * (row - 2) + pair - 1])
    for side in range(2):

        @pl.when(place[0] == side)
        def _():
            for base, buffer in ((4 - 4 * side, paired_rows), (4 * side, across_rows)):
                for row in range(2):
                    for pair in (1, 2):
                        start = 128 * (2 * row + pair - 1)
                        put(base + row, pair, buffer[ROW_POLES:ROW_ALL, start : start + 128])

        @pl.when(place[1] == side)
        def _():
            for pair, buffer in ((3 - 3 * side, paired_cols), (3 * side, across_cols)):
                for row in range(6):
                    base, lane = COL_POLES + 32 * (row // 2), 256 * (row % 2)
                    put(row, pair, unflat(buffer[base : base + 32, lane : lane + 256]))

    low1, low2 = place[1] == 0, place[5] == 0
    for row in range(5):
        base, lane = 16 * (row // 2), 256 * (row % 2)
        pair_1 = paired_cols[COL_BOX + base : COL_BOX + base + 16, lane : lane + 256]
        across_1 = across_cols[COL_BOX + base : COL_BOX + base + 16, lane : lane + 256]
        pair_2, across_2 = [ref[base : base + 16, lane : lane + 256] for ref in (pair2, across2)]
        found = (
            jnp.where(low2, across_2, pair_2),
            jnp.where(low1, across_1, pair_1),
            boxes[base : base + 16, lane : lane + 256],
            jnp.where(low1, pair_1, across_1),
            jnp.where(low2, pair_2, across_2),
        )
        for col in range(5):
            start = 64 * (5 * row + col)
            window[start : start + 64, :] = unfold(unflat(found[col]))
    spread = flag_row(flags[...])
    for row in range(2):
        for col in range(4):
            leaf = 4 * row + col
            seen = jnp.concatenate([table[row + a, 64 * col : 64 * (col + 5), :] for a in range(5)], axis=0)
            local[leaf] = box_product(coupling[leaf], spread[leaf : leaf + 1], seen).astype(BF16)
    box_out[...] = box_product(box_coupling[0], spread[8:9], window[...])
    for leaf in range(8):
        moved = lax.dot_general(transfer[leaf], basis[leaf], TN, preferred_element_type=F32)
        moved_basis[leaf] = moved.astype(BF16)
    for leaf in range(8):
        far = lax.dot_general(local[leaf], basis[leaf], TN, preferred_element_type=F32)
        out[leaf] = acc[leaf] + far


def last_kernel(
    near, box_one, flags, box_coupling, moved_basis,
    sums, pair2, across2, boxes3, pair4, across4, pair8,
    out_hbm, window, out, sems,
):
    place = place_bits()
    spread = flag_row(flags[...])
    total = box_one[...]
    low2, low4, low8 = place[5] == 0, place[6] == 0, place[7] == 0
    blank = jnp.zeros((16, 256), BF16)
    for level in range(2):
        lanes = slice(256 * level, 256 * level + 256)
        for row in range(5):
            rows = slice(16 * row, 16 * row + 16)
            later = slice(48 + 16 * row, 64 + 16 * row)
            pair_4, across_4 = pair4[rows, lanes], across4[rows, lanes]
            minus4, plus4 = jnp.where(low4, across_4, pair_4), jnp.where(low4, pair_4, across_4)
            if level == 0:
                pair_2, across_2 = pair2[later, lanes], across2[later, lanes]
                minus2, plus2 = jnp.where(low2, across_2, pair_2), jnp.where(low2, pair_2, across_2)
                found = (minus4, minus2, sums[rows, lanes], plus2, plus4)
            else:
                far = pair8[rows, :]
                found = (jnp.where(low8, blank, far), minus4, boxes3[rows, :], plus4, jnp.where(low8, far, blank))
            for col in range(5):
                start = 64 * (5 * row + col)
                window[start : start + 64, :] = unfold(unflat(found[col]))
        total = total + box_product(box_coupling[1 + level], spread[9 + level : 10 + level], window[...])
    total = total.T.astype(BF16)
    stores = [pltpu.make_async_copy(out.at[leaf], out_hbm.at[leaf], sems.at[leaf]) for leaf in range(8)]
    for leaf in range(8):
        far = jnp.dot(total, moved_basis[leaf], preferred_element_type=F32)
        out[leaf] = (near[leaf] + far).astype(BF16)
        stores[leaf].start()
    for store in stores:
        store.wait()


def near_scratch(sources):
    return [
        pltpu.SMEM((32,), jnp.int32),
        pltpu.VMEM((8, 8, PANELS), F32),
        *([pltpu.VMEM((8, LOADS, PANELS), BF16)] if sources else []),
        pltpu.VMEM((8, LOADS, PANELS), F32),
    ]


def body(
    charges,
    offsets,
    leaf_basis,
    near_mask,
    leaf_coupling,
    leaf_distant_flags,
    leaf_transfer,
    box_coupling,
    box_far,
    parent_child_transfer,
):
    charges = charges.reshape(8, LOADS, PANELS)
    offsets = offsets.transpose(0, 2, 1, 3)
    basis = leaf_basis.reshape(8, RANK, PANELS)
    mask = near_mask.reshape(8, 8)
    coupling = leaf_coupling.reshape(8, RANK, WIDE)
    transfer = leaf_transfer.reshape(8, RANK, RANK)
    box_coupling = box_coupling.reshape(3, RANK, WIDE)
    parent = parent_child_transfer.reshape(2, RANK, RANK)
    flags = jnp.concatenate([leaf_distant_flags.reshape(8, 25), box_far.reshape(3, 25)], axis=0)
    flags = jnp.pad(flags, ((0, 5), (0, 7))).astype(BF16)
    near_cost = 6 * 10**9
    rows_pair, rows_across, small, poles, feats = kernel_call(
        first_kernel,
        (shape((ROW_ALL, 512)), shape((ROW_ALL, 512)), shape((3, 32, 128)), shape((4, 64, 128)), shape((8, PANELS, 16))),
        [
            pltpu.VMEM((8, LOADS, PANELS), BF16),
            pltpu.VMEM((2, 3, 4, PANELS), BF16),
            pltpu.VMEM((8, RANK, PANELS), BF16),
            pltpu.VMEM((8, RANK, RANK), BF16),
            pltpu.VMEM((2, RANK, RANK), BF16),
            pltpu.SemaphoreType.DMA((11,)),
        ],
        "first", 10**9, charges, offsets, basis, transfer, parent, hbm=(0, 1, 2, 3, 4),
    )

    pair1 = paired(small, "row", 1)
    paired_rows = paired(rows_pair, "row", 1)
    near_args = (mask, charges, offsets, feats)

    def inner_call(targets, name, after):
        return kernel_call(
            functools.partial(inner_kernel, targets), shape((len(targets), LOADS, PANELS), F32),
            near_scratch(False), name, near_cost, *near_args, smem=(0,), after=after,
        )

    halves = (small[1:3].astype(F32) + pair1[1:3].astype(F32)).astype(BF16)
    payload = jnp.concatenate([small[:1], pair1[:1], halves], axis=0)
    pair2 = paired(payload, "row", 2)
    inner0 = inner_call((0, 1, 2), "inner0", (payload,))
    pair2, inner0 = lax.optimization_barrier((pair2, inner0))
    quarter = (small[2].astype(F32) + pair1[2].astype(F32) + pair2[3].astype(F32)).astype(BF16)
    payload = jnp.concatenate([pair2[2:3], quarter[None], small[:1], pair1[:1], halves[:1]], axis=0)
    pair4 = paired(payload, "row", 6)
    payload, rows_across = lax.optimization_barrier((payload, rows_across))
    across_rows = paired_across(rows_across, "row", 1)
    inner1 = inner_call((3, 4, 5), "inner1", (payload,))
    pair4, inner1 = lax.optimization_barrier((pair4, inner1))
    payload = jnp.concatenate([quarter[None], pair4[1:2], pair4[0:1], pair4[2:5]], axis=0)
    pair8, across8 = paired(payload, "row", 8), paired_across(payload, "row", 8)
    by_rows = kernel_call(
        row_kernel, shape((8, LOADS, PANELS), F32), near_scratch(True), "byrows", near_cost,
        mask, feats, paired_rows, across_rows, smem=(0,), after=(payload,),
    )

    pair8, across8, by_rows = lax.optimization_barrier((pair8, across8, by_rows))

    cols_pair, cols_across, boxes1, row_sums = kernel_call(
        pack_kernel,
        (shape((COL_ALL + SUMS, 512)), shape((COL_ALL, 512)), shape((48, 512)), shape((SUMS, 512))),
        [], "pack", 10**8, charges, offsets, poles, paired_rows, across_rows,
        small, pair1, pair2, pair4, pair8, across8,
    )
    paired_cols = paired(cols_pair, "col", 1)
    across_cols = paired_across(cols_across, "col", 1)
    sums = (row_sums.astype(F32) + paired_cols[COL_ALL:].astype(F32)).astype(BF16)
    payload = jnp.concatenate([boxes1, sums], axis=0)
    col_pair2, col_across2 = paired(payload, "col", 2), paired_across(payload, "col", 2)
    inner2 = inner_call((6, 7), "inner2", (payload,))
    col_pair2, inner2 = lax.optimization_barrier((col_pair2, inner2))
    boxes3 = (sums[:, 256:].astype(F32) + col_pair2[48:, 256:].astype(F32)).astype(BF16)
    payload = jnp.concatenate([sums[:, :256], boxes3], axis=1)
    col_pair4, col_across4 = paired(payload, "col", 4), paired_across(payload, "col", 4)
    col_pair8 = paired(boxes3, "col", 10)
    direct, box_one, moved_basis = kernel_call(
        edge_kernel,
        (shape((8, LOADS, PANELS), F32), shape((RANK, LOADS), F32), shape((8, RANK, PANELS))),
        near_scratch(True)
        + [pltpu.VMEM((6, 512, LOADS), BF16), pltpu.VMEM((WIDE, LOADS), BF16), pltpu.VMEM((8, RANK, LOADS), BF16)],
        "edge", near_cost, mask, feats, paired_cols, across_cols, inner0, inner1, inner2, by_rows, poles,
        paired_rows, across_rows, flags, coupling, box_coupling, boxes1, col_pair2, col_across2, transfer, basis,
        smem=(0,), after=(payload,),
    )
    out = kernel_call(
        last_kernel, shape((8, LOADS, PANELS)),
        [pltpu.VMEM((WIDE, LOADS), BF16), pltpu.VMEM((8, LOADS, PANELS), BF16), pltpu.SemaphoreType.DMA((8,))], "last", 10**9,
        direct, box_one, flags, box_coupling, moved_basis,
        sums, col_pair2, col_across2, boxes3, col_pair4, col_across4, col_pair8, out_space=HBM,
    )
    return out.reshape(2, 4, LOADS, PANELS)


def solution(mesh):
    return jax.shard_map(
        body,
        mesh=mesh,
        in_specs=(
            P("row", "col", None, None),
            P("row", "col", None, None),
            P("row", "col", None, None),
            P("row", "col", None),
            P("row", "col", None, None),
            P("row", "col", None),
            P("row", "col", None, None),
            P("row", "col", None, None, None),
            P("row", "col", None, None),
            P("row", "col", None, None, None),
        ),
        out_specs=P("row", "col", None, None),
        check_vma=False,
    )
```

```python
import functools

import jax
import jax.numpy as jnp
from jax import lax
from jax.experimental import pallas as pl
from jax.experimental.pallas import tpu as pltpu
from jax.sharding import PartitionSpec as P

PANELS = 512
RANK = 64
LOADS = 64
EPSILON = 0.001
F32 = jnp.float32
BF16 = jnp.bfloat16
NT = (((1,), (1,)), ((), ()))
TN = (((0,), (0,)), ((), ()))
WIDE = 25 * RANK
MIB = 2**20
AT_ONCE = (8, 4, 2, 1)
VMEM = pl.BlockSpec(memory_space=pltpu.VMEM)
SMEM = pl.BlockSpec(memory_space=pltpu.SMEM)
HBM = pl.BlockSpec(memory_space=pltpu.HBM)

ROW_OFFS, ROW_POLES, ROW_ALL = 256, 272, 336
COL_OFFS, COL_POLES, COL_BOX, COL_ALL = 256, 272, 368, 416
SUMS = 80


def paired(value, axis, distance):
    return lax.ppermute(value, axis, [(i, i ^ distance) for i in range(lax.axis_size(axis))])


def paired_across(value, axis, distance):
    count = lax.axis_size(axis)
    moves = [(i, i + distance if i & distance else i - distance) for i in range(count)]
    return lax.ppermute(value, axis, [(i, j) for i, j in moves if 0 <= j < count])


def kernel_call(body, outs, scratch, name, cost, *args, smem=(), hbm=(), after=(), out_space=VMEM):
    count = len(args)

    def with_order(*refs):
        body(*refs[:count], *refs[count + len(after) :])

    spaces = [SMEM if i in smem else HBM if i in hbm else VMEM for i in range(count)]
    return pl.pallas_call(
        with_order,
        out_shape=outs,
        in_specs=spaces + [VMEM] * len(after),
        out_specs=jax.tree.map(lambda _: out_space, outs),
        scratch_shapes=scratch,
        compiler_params=pltpu.CompilerParams(vmem_limit_bytes=40 * MIB),
        cost_estimate=pl.CostEstimate(flops=cost, bytes_accessed=4 * MIB, transcendentals=0),
        name=name,
    )(*[pltpu.with_memory_space_constraint(arg, pltpu.HBM) if i in hbm else arg for i, arg in enumerate(args)], *after)


def shape(dims, dtype=BF16):
    return jax.ShapeDtypeStruct(dims, dtype)


def fold(matrix):
    return jnp.concatenate([matrix[:32], matrix[32:]], axis=1)


def unfold(folded):
    return jnp.concatenate([folded[:, :64], folded[:, 64:]], axis=0)


def place_bits():
    row, col = lax.axis_index("row"), lax.axis_index("col")
    return [value & 1 for value in (row, col, row >> 1, row >> 2, row >> 3, col >> 1, col >> 2, col >> 3)]


def flat(folded):
    return jnp.concatenate([folded[:16], folded[16:]], axis=1)


def unflat(flattened):
    return jnp.concatenate([flattened[:, :128], flattened[:, 128:]], axis=0)


def rows_of(values, count):
    row = lax.broadcasted_iota(jnp.int32, (count, PANELS), 0)
    out = jnp.zeros((count, PANELS), F32)
    for index, value in enumerate(values):
        out = jnp.where(row == index, value, out)
    return out


def three_parts(value):
    high = value.astype(BF16).astype(F32)
    rest = value - high
    middle = rest.astype(BF16).astype(F32)
    low = (rest - middle).astype(BF16).astype(F32)
    return high, middle, low


def target_features(off):
    x, y, z = off
    high, middle, low = three_parts(PANELS * (x * x + y * y + z * z + EPSILON))
    return rows_of([x, y, z, x, y, high, middle, low, 1.0, 1.0, 1.0], 16).T.astype(BF16)


def source_features(off, row_off, col_off):
    x, y, z = off[0:1], off[1:2], off[2:3]
    x_moved, y_moved = x + col_off, y + row_off
    high, middle, low = three_parts(PANELS * (x_moved * x_moved + y_moved * y_moved + z * z))
    twice = -2.0 * PANELS
    return rows_of(
        [twice * x, twice * y, twice * z, twice * col_off, twice * row_off, 1.0, 1.0, 1.0, high, middle, low], 16
    ).astype(BF16)


def near_pairs(pairs, mask_copy, mask, listed, target_feats, source_offs, source_charges, acc):
    mask_copy.wait()
    count = jnp.int32(0)
    for target, slot, source, row_off, col_off in pairs:
        listed[count] = target + 16 * source + 256 * (row_off + 1) + 1024 * (col_off + 1)
        count = count + (1 if slot is None else mask[target, slot])

    def one(index):
        code = listed[index]
        target = code & 15
        source = (code >> 4) & 15
        row_off = ((code >> 8) & 3) - 1
        col_off = ((code >> 10) & 3) - 1
        moved = source_features(source_offs[source, 0:3, :], row_off.astype(F32), col_off.astype(F32))
        squared = jnp.dot(target_feats[target], moved, preferred_element_type=F32)
        tile = lax.rsqrt(squared).astype(BF16)
        acc[target] += lax.dot_general(source_charges[source], tile, NT, preferred_element_type=F32)

    done = jnp.int32(0)
    for at_once in AT_ONCE:
        steps = (count - done) // at_once

        def several(step, carry, done=done, at_once=at_once):
            for k in range(at_once):
                one(done + step * at_once + k)
            return carry

        lax.fori_loop(0, steps, several, 0)
        done = done + steps * at_once


def slot_of(row_off, col_off):
    place = 3 * (row_off + 1) + col_off + 1
    return None if place == 4 else place - (place > 4)


def inner_pairs(targets):
    found = []
    for target in targets:
        row, col = divmod(target, 4)
        for row_off in (-1, 0, 1):
            for col_off in (-1, 0, 1):
                at_row, at_col = row + row_off, col + col_off
                if 0 <= at_row < 2 and 0 <= at_col < 4:
                    found.append((target, slot_of(row_off, col_off), 4 * at_row + at_col, row_off, col_off))
    return found


def row_pairs():
    found = []
    for row, row_off in ((0, -1), (1, 1)):
        for col in range(4):
            for col_off in (-1, 0, 1):
                if 0 <= col + col_off < 4:
                    found.append((4 * row + col, slot_of(row_off, col_off), 4 * row + col + col_off, row_off, col_off))
    return found


def col_pairs():
    found = []
    for side, col, col_off in ((0, 0, -1), (1, 3, 1)):
        for row in range(2):
            for row_off in (-1, 0, 1):
                found.append((4 * row + col, slot_of(row_off, col_off), 4 * side + row + row_off + 1, row_off, col_off))
    return found


def first_kernel(
    charges_hbm, offsets_hbm, basis_hbm, transfer_hbm, parent_hbm,
    with_pair, across, small, poles_out, feats,
    charges, offsets, basis, transfer, parent, sems,
):
    side = place_bits()[0]
    loads = []
    for k in range(4):
        rows = pl.ds(2 * k, 2)
        loads.append(pltpu.make_async_copy(charges_hbm.at[rows], charges.at[rows], sems.at[k]))
        loads.append(pltpu.make_async_copy(basis_hbm.at[rows], basis.at[rows], sems.at[4 + k]))
    loads.append(pltpu.make_async_copy(transfer_hbm, transfer, sems.at[8]))
    loads.append(pltpu.make_async_copy(parent_hbm, parent, sems.at[9]))
    load_offsets = pltpu.make_async_copy(offsets_hbm, offsets, sems.at[10])
    load_offsets.start()
    for load in loads:
        load.start()
    load_offsets.wait()
    offs = [[offsets[row, k].astype(F32) for k in range(3)] for row in range(2)]
    halves = [rows_of([offs[row][k % 3][k // 3 : k // 3 + 1] for k in range(12)], 16).astype(BF16) for row in range(2)]
    with_pair[ROW_OFFS:ROW_POLES, :] = jnp.where(side == 0, halves[1], halves[0])
    across[ROW_OFFS:ROW_POLES, :] = jnp.where(side == 0, halves[0], halves[1])
    for leaf in range(8):
        row, col = divmod(leaf, 4)
        feats[leaf] = target_features([offs[row][k][col : col + 1] for k in range(3)])
    poles = []
    for k in range(4):
        loads[2 * k].wait()
        loads[2 * k + 1].wait()
        for leaf in (2 * k, 2 * k + 1):
            poles.append(lax.dot_general(basis[leaf], charges[leaf], NT, preferred_element_type=F32).astype(BF16))
    loads[8].wait()
    box = jnp.zeros((RANK, LOADS), F32)
    for leaf in range(8):
        box = box + lax.dot_general(transfer[leaf], poles[leaf], TN, preferred_element_type=F32)
    box = box.astype(BF16)
    small[0] = fold(box)
    loads[9].wait()
    for level in range(2):
        term = lax.dot_general(parent[level], box, TN, preferred_element_type=F32)
        small[1 + level] = fold(term.astype(BF16))
    pairs = [jnp.concatenate([poles[2 * k], poles[2 * k + 1]], axis=1) for k in range(4)]
    for k in range(4):
        poles_out[k] = pairs[k]
    for buffer, row in ((with_pair, 1 - side), (across, side)):
        for col in range(4):
            buffer[64 * col : 64 * (col + 1), :] = charges[4 * row + col]
        for k in range(4):
            buffer[ROW_POLES:ROW_ALL, 128 * k : 128 * (k + 1)] = pairs[k]


def own_offsets(offsets, offs):
    for row in range(2):
        for k in range(3):
            values = offsets[row, k].astype(F32)
            for col in range(4):
                offs[4 * row + col, k : k + 1, :] = values[col : col + 1]


def inner_kernel(targets, mask_in, charges, offsets, feats, out, mask, sem, listed, offs, acc):
    mask_copy = pltpu.make_async_copy(mask_in, mask, sem)
    mask_copy.start()
    own_offsets(offsets, offs)
    for target in targets:
        acc[target] = jnp.zeros((LOADS, PANELS), F32)
    near_pairs(inner_pairs(targets), mask_copy, mask, listed, feats, offs, charges, acc)
    out[...] = acc[targets[0] : targets[-1] + 1]


def earliness():
    row = lax.axis_index("row")
    return jnp.where(row & 7 == 0, 2, jnp.where(row & 4 == 0, 1, 0))


def early_inner_kernel(mask_in, charges, offsets, feats, out, *scratch):
    ahead = earliness()
    for count, targets in enumerate(((0, 1, 2), (0, 1, 2, 3, 4, 5), (0, 1, 2, 3, 4, 5, 6, 7))):

        @pl.when(ahead == count)
        def _():
            inner_kernel(targets, mask_in, charges, offsets, feats, out.at[0 : len(targets)], *scratch)


def late_inner_kernel(targets, limit, *refs):
    @pl.when(earliness() < limit)
    def _():
        inner_kernel(targets, *refs)


def inner_basis_kernel(mask_in, charges, offsets, feats, transfer, basis, out, moved_basis, *scratch):
    for leaf in range(8):
        moved = lax.dot_general(transfer[leaf], basis[leaf], TN, preferred_element_type=F32)
        moved_basis[leaf] = moved.astype(BF16)
    late_inner_kernel((6, 7), 2, mask_in, charges, offsets, feats, out, *scratch)


def spread_offsets(packed, offs, base):
    values = packed.astype(F32)
    for leaf in range(4):
        offs[base + leaf, 0:3, :] = values[3 * leaf : 3 * leaf + 3]


def row_kernel(mask_in, feats, paired_rows, across_rows, out, mask, sem, listed, offs, charges, acc):
    mask_copy = pltpu.make_async_copy(mask_in, mask, sem)
    mask_copy.start()
    place = place_bits()
    for side, buffer in ((1 - place[0], paired_rows), (place[0], across_rows)):
        spread_offsets(buffer[ROW_OFFS:ROW_POLES, :], offs, 4 * side)
        for col in range(4):
            charges[4 * side + col] = buffer[64 * col : 64 * (col + 1), :]
    acc[...] = jnp.zeros_like(acc)
    near_pairs(row_pairs(), mask_copy, mask, listed, feats, offs, charges, acc)
    out[...] = acc[...]


def pack_kernel(
    charges, offsets, poles, paired_rows, across_rows, small, pair1, pair2, pair4, pair8, across8,
    with_pair, across, boxes_out, sums_out,
):
    place = place_bits()
    bit0, bit1, bit2 = place[0], place[2], place[3]
    at = bit0 == 0
    minus8, plus8 = [[jnp.where(place[4] == want, pair8[k], across8[k]) for k in range(6)] for want in (1, 0)]
    low2, low4 = bit1 == 0, bit2 == 0
    minus2, plus2 = [], []
    for k in range(3):
        other = jnp.where(low2 != low4, pair4[2 + k], jnp.where(low2, minus8[3 + k], plus8[3 + k]))
        minus2.append(jnp.where(low2, other, pair2[k]))
        plus2.append(jnp.where(low2, pair2[k], other))
    boxes = [
        minus2[0],
        jnp.where(at, minus2[1], pair1[0]),
        small[0],
        jnp.where(at, pair1[0], plus2[1]),
        plus2[0],
    ]
    own2 = (small[1].astype(F32) + pair1[1].astype(F32)).astype(BF16)
    own3 = (small[2].astype(F32) + pair1[2].astype(F32) + pair2[3].astype(F32)).astype(BF16)
    second = [
        jnp.where(low4, minus8[2], pair4[0]),
        minus2[2],
        own2,
        plus2[2],
        jnp.where(low4, pair4[0], plus8[2]),
    ]
    third = [
        minus8[0],
        jnp.where(low4, minus8[1], pair4[1]),
        own3,
        jnp.where(low4, pair4[1], plus8[1]),
        plus8[0],
    ]
    for row in range(5):
        base, lane = 16 * (row // 2), 256 * (row % 2)
        piece = flat(boxes[row])
        boxes_out[base : base + 16, lane : lane + 256] = piece
        for buffer in (with_pair, across):
            buffer[COL_BOX + base : COL_BOX + base + 16, lane : lane + 256] = piece
        for half, found in enumerate((second, third)):
            piece = flat(found[row])
            sums_out[16 * row : 16 * row + 16, 256 * half : 256 * half + 256] = piece
            with_pair[COL_ALL + 16 * row : COL_ALL + 16 * row + 16, 256 * half : 256 * half + 256] = piece
    blank = jnp.zeros((16, 256), BF16)
    boxes_out[32:48, 256:512] = blank
    for buffer in (with_pair, across):
        buffer[COL_BOX + 32 : COL_ALL, 256:512] = blank

    def fill(buffer, col, top, bottom):
        pair = col // 2
        offs = []
        for spot, source in enumerate((top, None, None, bottom)):
            if source is None:
                leaf = 4 * (spot - 1) + col
                buffer[64 * spot : 64 * (spot + 1), :] = charges[leaf]
                offs += [offsets[spot - 1, k].astype(F32)[col : col + 1] for k in range(3)]
            else:
                buffer[64 * spot : 64 * (spot + 1), :] = source[64 * col : 64 * (col + 1), :]
                off = source[ROW_OFFS:ROW_POLES, :].astype(F32)[3 * col : 3 * col + 3]
                offs += [off[0:1], off[1:2], off[2:3]]
        buffer[COL_OFFS:COL_POLES, :] = rows_of(offs, 16).astype(BF16)
        for row in range(6):
            if row in (2, 3):
                pole = poles[2 * (row - 2) + pair]
            else:
                source = top if row < 2 else bottom
                start = 128 * (2 * (row % 4) + pair)
                pole = source[ROW_POLES:ROW_ALL, start : start + 128]
            base, lane = COL_POLES + 32 * (row // 2), 256 * (row % 2)
            buffer[base : base + 32, lane : lane + 128] = pole[:32]
            buffer[base : base + 32, lane + 128 : lane + 256] = pole[32:]

    for row_side in range(2):
        for col_side in range(2):

            @pl.when((place[0] == row_side) & (place[1] == col_side))
            def _():
                top, bottom = (across_rows, paired_rows) if row_side == 0 else (paired_rows, across_rows)
                fill(with_pair, 0 if col_side else 3, top, bottom)
                fill(across, 3 if col_side else 0, top, bottom)


def flag_row(flags):
    row = lax.broadcasted_iota(jnp.int32, (32, WIDE), 0)
    lane = lax.broadcasted_iota(jnp.int32, (32, WIDE), 1)
    spread = jnp.where((lane >> 6) == row, 1.0, 0.0).astype(BF16)
    return jnp.dot(flags, spread, preferred_element_type=F32).astype(BF16)


def box_product(coupling, flags, window):
    return jnp.dot(coupling * flags, window, preferred_element_type=F32)


def edge_kernel(
    mask_in, feats, paired_cols, across_cols, inner0, inner1, inner2, by_rows, poles, paired_rows, across_rows, flags, coupling,
    box_coupling, boxes, pair2, across2, basis,
    out, box_out, mask, sem, listed, offs, charges, acc, table, window, local,
):
    mask_copy = pltpu.make_async_copy(mask_in, mask, sem)
    mask_copy.start()
    place = place_bits()
    for side, buffer in ((1 - place[1], paired_cols), (place[1], across_cols)):
        spread_offsets(buffer[COL_OFFS:COL_POLES, :], offs, 4 * side)
        for spot in range(4):
            charges[4 * side + spot] = buffer[64 * spot : 64 * (spot + 1), :]
    acc[0:3] = inner0[0:3] + by_rows[0:3]

    for first, last, late, limit in ((3, 6, inner1, 1), (6, 8, inner2, 2)):

        @pl.when(earliness() >= limit)
        def _():
            acc[first:last] = inner0[first:last] + by_rows[first:last]

        @pl.when(earliness() < limit)
        def _():
            acc[first:last] = late[...] + by_rows[first:last]


    def put(row, pair, both):
        table[row, 128 * pair : 128 * pair + 64, :] = both[:, :64]
        table[row, 128 * pair + 64 : 128 * pair + 128, :] = both[:, 64:]

    for row in (2, 3):
        for pair in (1, 2):
            put(row, pair, poles[2 * (row - 2) + pair - 1])
    for side in range(2):

        @pl.when(place[0] == side)
        def _():
            for base, buffer in ((4 - 4 * side, paired_rows), (4 * side, across_rows)):
                for row in range(2):
                    for pair in (1, 2):
                        start = 128 * (2 * row + pair - 1)
                        put(base + row, pair, buffer[ROW_POLES:ROW_ALL, start : start + 128])

        @pl.when(place[1] == side)
        def _():
            for pair, buffer in ((3 - 3 * side, paired_cols), (3 * side, across_cols)):
                for row in range(6):
                    base, lane = COL_POLES + 32 * (row // 2), 256 * (row % 2)
                    put(row, pair, unflat(buffer[base : base + 32, lane : lane + 256]))

    low1, low2 = place[1] == 0, place[5] == 0
    for row in range(5):
        base, lane = 16 * (row // 2), 256 * (row % 2)
        pair_1 = paired_cols[COL_BOX + base : COL_BOX + base + 16, lane : lane + 256]
        across_1 = across_cols[COL_BOX + base : COL_BOX + base + 16, lane : lane + 256]
        pair_2, across_2 = [ref[base : base + 16, lane : lane + 256] for ref in (pair2, across2)]
        found = (
            jnp.where(low2, across_2, pair_2),
            jnp.where(low1, across_1, pair_1),
            boxes[base : base + 16, lane : lane + 256],
            jnp.where(low1, pair_1, across_1),
            jnp.where(low2, pair_2, across_2),
        )
        for col in range(5):
            start = 64 * (5 * row + col)
            window[start : start + 64, :] = unfold(unflat(found[col]))
    spread = flag_row(flags[...])
    for row in range(2):
        for col in range(4):
            leaf = 4 * row + col
            seen = jnp.concatenate([table[row + a, 64 * col : 64 * (col + 5), :] for a in range(5)], axis=0)
            local[leaf] = box_product(coupling[leaf], spread[leaf : leaf + 1], seen).astype(BF16)
    box_out[...] = box_product(box_coupling[0], spread[8:9], window[...])
    near_pairs(col_pairs(), mask_copy, mask, listed, feats, offs, charges, acc)
    for leaf in range(8):
        far = lax.dot_general(local[leaf], basis[leaf], TN, preferred_element_type=F32)
        out[leaf] = acc[leaf] + far


def last_kernel(
    near, box_one, flags, box_coupling, moved_basis,
    sums, pair2, across2, boxes3, pair4, across4, pair8,
    out_hbm, window, out, sems,
):
    place = place_bits()
    spread = flag_row(flags[...])
    total = box_one[...]
    low2, low4, low8 = place[5] == 0, place[6] == 0, place[7] == 0
    blank = jnp.zeros((16, 256), BF16)
    for level in range(2):
        lanes = slice(256 * level, 256 * level + 256)
        for row in range(5):
            rows = slice(16 * row, 16 * row + 16)
            later = slice(48 + 16 * row, 64 + 16 * row)
            pair_4, across_4 = pair4[rows, lanes], across4[rows, lanes]
            minus4, plus4 = jnp.where(low4, across_4, pair_4), jnp.where(low4, pair_4, across_4)
            if level == 0:
                pair_2, across_2 = pair2[later, lanes], across2[later, lanes]
                minus2, plus2 = jnp.where(low2, across_2, pair_2), jnp.where(low2, pair_2, across_2)
                found = (minus4, minus2, sums[rows, lanes], plus2, plus4)
            else:
                far = pair8[rows, :]
                found = (jnp.where(low8, blank, far), minus4, boxes3[rows, :], plus4, jnp.where(low8, far, blank))
            for col in range(5):
                start = 64 * (5 * row + col)
                window[start : start + 64, :] = unfold(unflat(found[col]))
        total = total + box_product(box_coupling[1 + level], spread[9 + level : 10 + level], window[...])
    total = total.T.astype(BF16)
    stores = [pltpu.make_async_copy(out.at[leaf], out_hbm.at[leaf], sems.at[leaf]) for leaf in range(8)]
    for leaf in range(8):
        far = jnp.dot(total, moved_basis[leaf], preferred_element_type=F32)
        out[leaf] = (near[leaf] + far).astype(BF16)
        stores[leaf].start()
    for store in stores:
        store.wait()


def near_scratch(sources):
    return [
        pltpu.SMEM((8, 8), jnp.int32),
        pltpu.SemaphoreType.DMA(()),
        pltpu.SMEM((32,), jnp.int32),
        pltpu.VMEM((8, 8, PANELS), F32),
        *([pltpu.VMEM((8, LOADS, PANELS), BF16)] if sources else []),
        pltpu.VMEM((8, LOADS, PANELS), F32),
    ]


def body(
    charges,
    offsets,
    leaf_basis,
    near_mask,
    leaf_coupling,
    leaf_distant_flags,
    leaf_transfer,
    box_coupling,
    box_far,
    parent_child_transfer,
):
    charges = charges.reshape(8, LOADS, PANELS)
    offsets = offsets.transpose(0, 2, 1, 3)
    basis = leaf_basis.reshape(8, RANK, PANELS)
    mask = near_mask.reshape(8, 8)
    coupling = leaf_coupling.reshape(8, RANK, WIDE)
    transfer = leaf_transfer.reshape(8, RANK, RANK)
    box_coupling = box_coupling.reshape(3, RANK, WIDE)
    parent = parent_child_transfer.reshape(2, RANK, RANK)
    flags = jnp.concatenate([leaf_distant_flags.reshape(8, 25), box_far.reshape(3, 25)], axis=0)
    flags = jnp.pad(flags, ((0, 5), (0, 7))).astype(BF16)
    near_cost = 6 * 10**9
    rows_pair, rows_across, small, poles, feats = kernel_call(
        first_kernel,
        (shape((ROW_ALL, 512)), shape((ROW_ALL, 512)), shape((3, 32, 128)), shape((4, 64, 128)), shape((8, PANELS, 16))),
        [
            pltpu.VMEM((8, LOADS, PANELS), BF16),
            pltpu.VMEM((2, 3, 4, PANELS), BF16),
            pltpu.VMEM((8, RANK, PANELS), BF16),
            pltpu.VMEM((8, RANK, RANK), BF16),
            pltpu.VMEM((2, RANK, RANK), BF16),
            pltpu.SemaphoreType.DMA((11,)),
        ],
        "first", 10**9, charges, offsets, basis, transfer, parent, hbm=(0, 1, 2, 3, 4),
    )

    pair1 = paired(small, "row", 1)
    paired_rows = paired(rows_pair, "row", 1)
    near_args = (mask, charges, offsets, feats)

    def inner_call(kernel, count, name, after):
        return kernel_call(
            kernel, shape((count, LOADS, PANELS), F32),
            near_scratch(False), name, near_cost, *near_args, after=after,
        )

    halves = (small[1:3].astype(F32) + pair1[1:3].astype(F32)).astype(BF16)
    payload = jnp.concatenate([small[:1], pair1[:1], halves], axis=0)
    pair2 = paired(payload, "row", 2)
    inner0 = inner_call(early_inner_kernel, 8, "inner0", (payload,))
    pair2, inner0 = lax.optimization_barrier((pair2, inner0))
    quarter = (small[2].astype(F32) + pair1[2].astype(F32) + pair2[3].astype(F32)).astype(BF16)
    payload = jnp.concatenate([pair2[2:3], quarter[None], small[:1], pair1[:1], halves[:1]], axis=0)
    pair4 = paired(payload, "row", 6)
    payload, rows_across = lax.optimization_barrier((payload, rows_across))
    across_rows = paired_across(rows_across, "row", 1)
    inner1 = inner_call(functools.partial(late_inner_kernel, (3, 4, 5), 1), 3, "inner1", (payload,))
    pair4, inner1 = lax.optimization_barrier((pair4, inner1))
    payload = jnp.concatenate([quarter[None], pair4[1:2], pair4[0:1], pair4[2:5]], axis=0)
    pair8, across8 = paired(payload, "row", 8), paired_across(payload, "row", 8)
    by_rows = kernel_call(
        row_kernel, shape((8, LOADS, PANELS), F32), near_scratch(True), "byrows", near_cost,
        mask, feats, paired_rows, across_rows, after=(payload,),
    )

    pair8, across8, by_rows = lax.optimization_barrier((pair8, across8, by_rows))

    cols_pair, cols_across, boxes1, row_sums = kernel_call(
        pack_kernel,
        (shape((COL_ALL + SUMS, 512)), shape((COL_ALL, 512)), shape((48, 512)), shape((SUMS, 512))),
        [], "pack", 10**8, charges, offsets, poles, paired_rows, across_rows,
        small, pair1, pair2, pair4, pair8, across8,
    )
    paired_cols = paired(cols_pair, "col", 1)
    across_cols = paired_across(cols_across, "col", 1)
    sums = (row_sums.astype(F32) + paired_cols[COL_ALL:].astype(F32)).astype(BF16)
    payload = jnp.concatenate([boxes1, sums], axis=0)
    col_pair2, col_across2 = paired(payload, "col", 2), paired_across(payload, "col", 2)
    inner2, moved_basis = kernel_call(
        inner_basis_kernel, (shape((2, LOADS, PANELS), F32), shape((8, RANK, PANELS))), near_scratch(False), "inner2",
        near_cost, *near_args, transfer, basis, after=(payload,),
    )
    col_pair2, inner2 = lax.optimization_barrier((col_pair2, inner2))
    boxes3 = (sums[:, 256:].astype(F32) + col_pair2[48:, 256:].astype(F32)).astype(BF16)
    payload = jnp.concatenate([sums[:, :256], boxes3], axis=1)
    col_pair4, col_across4 = paired(payload, "col", 4), paired_across(payload, "col", 4)
    col_pair8 = paired(boxes3, "col", 10)
    direct, box_one = kernel_call(
        edge_kernel,
        (shape((8, LOADS, PANELS), F32), shape((RANK, LOADS), F32)),
        near_scratch(True)
        + [pltpu.VMEM((6, 512, LOADS), BF16), pltpu.VMEM((WIDE, LOADS), BF16), pltpu.VMEM((8, RANK, LOADS), BF16)],
        "edge", near_cost, mask, feats, paired_cols, across_cols, inner0, inner1, inner2, by_rows, poles,
        paired_rows, across_rows, flags, coupling, box_coupling, boxes1, col_pair2, col_across2, basis,
        after=(payload,),
    )
    out = kernel_call(
        last_kernel, shape((8, LOADS, PANELS)),
        [pltpu.VMEM((WIDE, LOADS), BF16), pltpu.VMEM((8, LOADS, PANELS), BF16), pltpu.SemaphoreType.DMA((8,))], "last", 10**9,
        direct, box_one, flags, box_coupling, moved_basis,
        sums, col_pair2, col_across2, boxes3, col_pair4, col_across4, col_pair8, out_space=HBM,
    )
    return out.reshape(2, 4, LOADS, PANELS)


def solution(mesh):
    return jax.shard_map(
        body,
        mesh=mesh,
        in_specs=(
            P("row", "col", None, None),
            P("row", "col", None, None),
            P("row", "col", None, None),
            P("row", "col", None),
            P("row", "col", None, None),
            P("row", "col", None),
            P("row", "col", None, None),
            P("row", "col", None, None, None),
            P("row", "col", None, None),
            P("row", "col", None, None, None),
        ),
        out_specs=P("row", "col", None, None),
        check_vma=False,
    )
```

```python
import functools

import jax
import jax.numpy as jnp
from jax import lax
from jax.experimental import pallas as pl
from jax.experimental.pallas import tpu as pltpu
from jax.sharding import PartitionSpec as P

PANELS = 512
RANK = 64
LOADS = 64
EPSILON = 0.001
F32 = jnp.float32
BF16 = jnp.bfloat16
NT = (((1,), (1,)), ((), ()))
TN = (((0,), (0,)), ((), ()))
WIDE = 25 * RANK
MIB = 2**20
AT_ONCE = (8, 4, 2, 1)
VMEM = pl.BlockSpec(memory_space=pltpu.VMEM)
SMEM = pl.BlockSpec(memory_space=pltpu.SMEM)
HBM = pl.BlockSpec(memory_space=pltpu.HBM)

ROW_OFFS, ROW_POLES, ROW_ALL = 256, 272, 336
COL_OFFS, COL_POLES, COL_BOX, COL_ALL = 256, 272, 368, 416
SUMS = 80


def paired(value, axis, distance):
    return lax.ppermute(value, axis, [(i, i ^ distance) for i in range(lax.axis_size(axis))])


def paired_across(value, axis, distance):
    count = lax.axis_size(axis)
    moves = [(i, i + distance if i & distance else i - distance) for i in range(count)]
    return lax.ppermute(value, axis, [(i, j) for i, j in moves if 0 <= j < count])


def kernel_call(body, outs, scratch, name, cost, *args, smem=(), hbm=(), after=(), out_space=VMEM):
    count = len(args)

    def with_order(*refs):
        body(*refs[:count], *refs[count + len(after) :])

    spaces = [SMEM if i in smem else HBM if i in hbm else VMEM for i in range(count)]
    return pl.pallas_call(
        with_order,
        out_shape=outs,
        in_specs=spaces + [VMEM] * len(after),
        out_specs=jax.tree.map(lambda _: out_space, outs),
        scratch_shapes=scratch,
        compiler_params=pltpu.CompilerParams(vmem_limit_bytes=40 * MIB),
        cost_estimate=pl.CostEstimate(flops=cost, bytes_accessed=4 * MIB, transcendentals=0),
        name=name,
    )(*[pltpu.with_memory_space_constraint(arg, pltpu.HBM) if i in hbm else arg for i, arg in enumerate(args)], *after)


def shape(dims, dtype=BF16):
    return jax.ShapeDtypeStruct(dims, dtype)


def fold(matrix):
    return jnp.concatenate([matrix[:32], matrix[32:]], axis=1)


def unfold(folded):
    return jnp.concatenate([folded[:, :64], folded[:, 64:]], axis=0)


def place_bits():
    row, col = lax.axis_index("row"), lax.axis_index("col")
    return [value & 1 for value in (row, col, row >> 1, row >> 2, row >> 3, col >> 1, col >> 2, col >> 3)]


def flat(folded):
    return jnp.concatenate([folded[:16], folded[16:]], axis=1)


def unflat(flattened):
    return jnp.concatenate([flattened[:, :128], flattened[:, 128:]], axis=0)


def rows_of(values, count):
    row = lax.broadcasted_iota(jnp.int32, (count, PANELS), 0)
    out = jnp.zeros((count, PANELS), F32)
    for index, value in enumerate(values):
        out = jnp.where(row == index, value, out)
    return out


def three_parts(value):
    high = value.astype(BF16).astype(F32)
    rest = value - high
    middle = rest.astype(BF16).astype(F32)
    low = (rest - middle).astype(BF16).astype(F32)
    return high, middle, low


def target_features(off):
    x, y, z = off
    high, middle, low = three_parts(PANELS * (x * x + y * y + z * z + EPSILON))
    return rows_of([x, y, z, x, y, high, middle, low, 1.0, 1.0, 1.0], 16).T.astype(BF16)


def source_features(off, row_off, col_off):
    x, y, z = off[0:1], off[1:2], off[2:3]
    x_moved, y_moved = x + col_off, y + row_off
    high, middle, low = three_parts(PANELS * (x_moved * x_moved + y_moved * y_moved + z * z))
    twice = -2.0 * PANELS
    return rows_of(
        [twice * x, twice * y, twice * z, twice * col_off, twice * row_off, 1.0, 1.0, 1.0, high, middle, low], 16
    ).astype(BF16)


def near_pairs(pairs, mask_copy, mask, listed, target_feats, source_offs, source_charges, acc):
    mask_copy.wait()
    count = jnp.int32(0)
    for target, slot, source, row_off, col_off in pairs:
        listed[count] = target + 16 * source + 256 * (row_off + 1) + 1024 * (col_off + 1)
        count = count + (1 if slot is None else mask[target, slot])

    def one(index):
        code = listed[index]
        target = code & 15
        source = (code >> 4) & 15
        row_off = ((code >> 8) & 3) - 1
        col_off = ((code >> 10) & 3) - 1
        moved = source_features(source_offs[source, 0:3, :], row_off.astype(F32), col_off.astype(F32))
        squared = jnp.dot(target_feats[target], moved, preferred_element_type=F32)
        tile = lax.rsqrt(squared).astype(BF16)
        acc[target] += lax.dot_general(source_charges[source], tile, NT, preferred_element_type=F32)

    done = jnp.int32(0)
    for at_once in AT_ONCE:
        steps = (count - done) // at_once

        def several(step, carry, done=done, at_once=at_once):
            for k in range(at_once):
                one(done + step * at_once + k)
            return carry

        lax.fori_loop(0, steps, several, 0)
        done = done + steps * at_once


def slot_of(row_off, col_off):
    place = 3 * (row_off + 1) + col_off + 1
    return None if place == 4 else place - (place > 4)


def inner_pairs(targets):
    found = []
    for target in targets:
        row, col = divmod(target, 4)
        for row_off in (-1, 0, 1):
            for col_off in (-1, 0, 1):
                at_row, at_col = row + row_off, col + col_off
                if 0 <= at_row < 2 and 0 <= at_col < 4:
                    found.append((target, slot_of(row_off, col_off), 4 * at_row + at_col, row_off, col_off))
    return found


def row_pairs():
    found = []
    for row, row_off in ((0, -1), (1, 1)):
        for col in range(4):
            for col_off in (-1, 0, 1):
                if 0 <= col + col_off < 4:
                    found.append((4 * row + col, slot_of(row_off, col_off), 4 * row + col + col_off, row_off, col_off))
    return found


def col_pairs():
    found = []
    for side, col, col_off in ((0, 0, -1), (1, 3, 1)):
        for row in range(2):
            for row_off in (-1, 0, 1):
                found.append((4 * row + col, slot_of(row_off, col_off), 4 * side + row + row_off + 1, row_off, col_off))
    return found


def first_kernel(
    charges_hbm, offsets_hbm, basis_hbm, transfer_hbm, parent_hbm,
    with_pair, across, small, poles_out, feats,
    charges, offsets, basis, transfer, parent, sems,
):
    side = place_bits()[0]
    loads = []
    for k in range(4):
        rows = pl.ds(2 * k, 2)
        loads.append(pltpu.make_async_copy(charges_hbm.at[rows], charges.at[rows], sems.at[k]))
        loads.append(pltpu.make_async_copy(basis_hbm.at[rows], basis.at[rows], sems.at[4 + k]))
    loads.append(pltpu.make_async_copy(transfer_hbm, transfer, sems.at[8]))
    loads.append(pltpu.make_async_copy(parent_hbm, parent, sems.at[9]))
    load_offsets = pltpu.make_async_copy(offsets_hbm, offsets, sems.at[10])
    load_offsets.start()
    for load in loads:
        load.start()
    load_offsets.wait()
    offs = [[offsets[row, k].astype(F32) for k in range(3)] for row in range(2)]
    halves = [rows_of([offs[row][k % 3][k // 3 : k // 3 + 1] for k in range(12)], 16).astype(BF16) for row in range(2)]
    with_pair[ROW_OFFS:ROW_POLES, :] = jnp.where(side == 0, halves[1], halves[0])
    across[ROW_OFFS:ROW_POLES, :] = jnp.where(side == 0, halves[0], halves[1])
    for leaf in range(8):
        row, col = divmod(leaf, 4)
        feats[leaf] = target_features([offs[row][k][col : col + 1] for k in range(3)])
    poles = []
    for k in range(4):
        loads[2 * k].wait()
        loads[2 * k + 1].wait()
        for leaf in (2 * k, 2 * k + 1):
            poles.append(lax.dot_general(basis[leaf], charges[leaf], NT, preferred_element_type=F32).astype(BF16))
    loads[8].wait()
    box = jnp.zeros((RANK, LOADS), F32)
    for leaf in range(8):
        box = box + lax.dot_general(transfer[leaf], poles[leaf], TN, preferred_element_type=F32)
    box = box.astype(BF16)
    small[0] = fold(box)
    loads[9].wait()
    for level in range(2):
        term = lax.dot_general(parent[level], box, TN, preferred_element_type=F32)
        small[1 + level] = fold(term.astype(BF16))
    pairs = [jnp.concatenate([poles[2 * k], poles[2 * k + 1]], axis=1) for k in range(4)]
    for k in range(4):
        poles_out[k] = pairs[k]
    for buffer, row in ((with_pair, 1 - side), (across, side)):
        for col in range(4):
            buffer[64 * col : 64 * (col + 1), :] = charges[4 * row + col]
        for k in range(4):
            buffer[ROW_POLES:ROW_ALL, 128 * k : 128 * (k + 1)] = pairs[k]


def own_offsets(offsets, offs):
    for row in range(2):
        for k in range(3):
            values = offsets[row, k].astype(F32)
            for col in range(4):
                offs[4 * row + col, k : k + 1, :] = values[col : col + 1]


def inner_kernel(targets, mask_in, charges, offsets, feats, out, mask, sem, listed, offs, acc):
    mask_copy = pltpu.make_async_copy(mask_in, mask, sem)
    mask_copy.start()
    own_offsets(offsets, offs)
    for target in targets:
        acc[target] = jnp.zeros((LOADS, PANELS), F32)
    near_pairs(inner_pairs(targets), mask_copy, mask, listed, feats, offs, charges, acc)
    out[...] = acc[targets[0] : targets[-1] + 1]


def earliness():
    row = lax.axis_index("row")
    return jnp.where(row & 7 == 0, 2, jnp.where(row & 4 == 0, 1, 0))


def early_inner_kernel(mask_in, charges, offsets, feats, out, *scratch):
    ahead = earliness()
    for count, targets in enumerate(((0, 1, 2), (0, 1, 2, 3, 4, 5), (0, 1, 2, 3, 4, 5, 6, 7))):

        @pl.when(ahead == count)
        def _():
            inner_kernel(targets, mask_in, charges, offsets, feats, out.at[0 : len(targets)], *scratch)


def late_inner_kernel(targets, limit, *refs):
    @pl.when(earliness() < limit)
    def _():
        inner_kernel(targets, *refs)


def basis_kernel(transfer, basis, out):
    for leaf in range(8):
        moved = lax.dot_general(transfer[leaf], basis[leaf], TN, preferred_element_type=F32)
        out[leaf] = moved.astype(BF16)


def spread_offsets(packed, offs, base):
    values = packed.astype(F32)
    for leaf in range(4):
        offs[base + leaf, 0:3, :] = values[3 * leaf : 3 * leaf + 3]


def row_kernel(mask_in, feats, paired_rows, across_rows, out, mask, sem, listed, offs, charges, acc):
    mask_copy = pltpu.make_async_copy(mask_in, mask, sem)
    mask_copy.start()
    place = place_bits()
    for side, buffer in ((1 - place[0], paired_rows), (place[0], across_rows)):
        spread_offsets(buffer[ROW_OFFS:ROW_POLES, :], offs, 4 * side)
        for col in range(4):
            charges[4 * side + col] = buffer[64 * col : 64 * (col + 1), :]
    acc[...] = jnp.zeros_like(acc)
    near_pairs(row_pairs(), mask_copy, mask, listed, feats, offs, charges, acc)
    out[...] = acc[...]


def pack_kernel(
    charges, offsets, poles, paired_rows, across_rows, small, pair1, pair2, pair4, pair8, across8,
    with_pair, across, boxes_out, sums_out,
):
    place = place_bits()
    bit0, bit1, bit2 = place[0], place[2], place[3]
    at = bit0 == 0
    minus8, plus8 = [[jnp.where(place[4] == want, pair8[k], across8[k]) for k in range(6)] for want in (1, 0)]
    low2, low4 = bit1 == 0, bit2 == 0
    minus2, plus2 = [], []
    for k in range(3):
        other = jnp.where(low2 != low4, pair4[2 + k], jnp.where(low2, minus8[3 + k], plus8[3 + k]))
        minus2.append(jnp.where(low2, other, pair2[k]))
        plus2.append(jnp.where(low2, pair2[k], other))
    boxes = [
        minus2[0],
        jnp.where(at, minus2[1], pair1[0]),
        small[0],
        jnp.where(at, pair1[0], plus2[1]),
        plus2[0],
    ]
    own2 = (small[1].astype(F32) + pair1[1].astype(F32)).astype(BF16)
    own3 = (small[2].astype(F32) + pair1[2].astype(F32) + pair2[3].astype(F32)).astype(BF16)
    second = [
        jnp.where(low4, minus8[2], pair4[0]),
        minus2[2],
        own2,
        plus2[2],
        jnp.where(low4, pair4[0], plus8[2]),
    ]
    third = [
        minus8[0],
        jnp.where(low4, minus8[1], pair4[1]),
        own3,
        jnp.where(low4, pair4[1], plus8[1]),
        plus8[0],
    ]
    for row in range(5):
        base, lane = 16 * (row // 2), 256 * (row % 2)
        piece = flat(boxes[row])
        boxes_out[base : base + 16, lane : lane + 256] = piece
        for buffer in (with_pair, across):
            buffer[COL_BOX + base : COL_BOX + base + 16, lane : lane + 256] = piece
        for half, found in enumerate((second, third)):
            piece = flat(found[row])
            sums_out[16 * row : 16 * row + 16, 256 * half : 256 * half + 256] = piece
            with_pair[COL_ALL + 16 * row : COL_ALL + 16 * row + 16, 256 * half : 256 * half + 256] = piece
    blank = jnp.zeros((16, 256), BF16)
    boxes_out[32:48, 256:512] = blank
    for buffer in (with_pair, across):
        buffer[COL_BOX + 32 : COL_ALL, 256:512] = blank

    def fill(buffer, col, top, bottom):
        pair = col // 2
        offs = []
        for spot, source in enumerate((top, None, None, bottom)):
            if source is None:
                leaf = 4 * (spot - 1) + col
                buffer[64 * spot : 64 * (spot + 1), :] = charges[leaf]
                offs += [offsets[spot - 1, k].astype(F32)[col : col + 1] for k in range(3)]
            else:
                buffer[64 * spot : 64 * (spot + 1), :] = source[64 * col : 64 * (col + 1), :]
                off = source[ROW_OFFS:ROW_POLES, :].astype(F32)[3 * col : 3 * col + 3]
                offs += [off[0:1], off[1:2], off[2:3]]
        buffer[COL_OFFS:COL_POLES, :] = rows_of(offs, 16).astype(BF16)
        for row in range(6):
            if row in (2, 3):
                pole = poles[2 * (row - 2) + pair]
            else:
                source = top if row < 2 else bottom
                start = 128 * (2 * (row % 4) + pair)
                pole = source[ROW_POLES:ROW_ALL, start : start + 128]
            base, lane = COL_POLES + 32 * (row // 2), 256 * (row % 2)
            buffer[base : base + 32, lane : lane + 128] = pole[:32]
            buffer[base : base + 32, lane + 128 : lane + 256] = pole[32:]

    for row_side in range(2):
        for col_side in range(2):

            @pl.when((place[0] == row_side) & (place[1] == col_side))
            def _():
                top, bottom = (across_rows, paired_rows) if row_side == 0 else (paired_rows, across_rows)
                fill(with_pair, 0 if col_side else 3, top, bottom)
                fill(across, 3 if col_side else 0, top, bottom)


def flag_row(flags):
    row = lax.broadcasted_iota(jnp.int32, (32, WIDE), 0)
    lane = lax.broadcasted_iota(jnp.int32, (32, WIDE), 1)
    spread = jnp.where((lane >> 6) == row, 1.0, 0.0).astype(BF16)
    return jnp.dot(flags, spread, preferred_element_type=F32).astype(BF16)


def box_product(coupling, flags, window):
    return jnp.dot(coupling * flags, window, preferred_element_type=F32)


def edge_kernel(
    mask_in, feats, paired_cols, across_cols, inner0, inner1, inner2, by_rows, poles, paired_rows, across_rows, flags, coupling,
    box_coupling, boxes, pair2, across2, basis,
    out, box_out, mask, sem, listed, offs, charges, acc, table, window, local,
):
    mask_copy = pltpu.make_async_copy(mask_in, mask, sem)
    mask_copy.start()
    place = place_bits()
    for side, buffer in ((1 - place[1], paired_cols), (place[1], across_cols)):
        spread_offsets(buffer[COL_OFFS:COL_POLES, :], offs, 4 * side)
        for spot in range(4):
            charges[4 * side + spot] = buffer[64 * spot : 64 * (spot + 1), :]
    acc[0:3] = inner0[0:3] + by_rows[0:3]

    for first, last, late, limit in ((3, 6, inner1, 1), (6, 8, inner2, 2)):

        @pl.when(earliness() >= limit)
        def _():
            acc[first:last] = inner0[first:last] + by_rows[first:last]

        @pl.when(earliness() < limit)
        def _():
            acc[first:last] = late[...] + by_rows[first:last]


    def put(row, pair, both):
        table[row, 128 * pair : 128 * pair + 64, :] = both[:, :64]
        table[row, 128 * pair + 64 : 128 * pair + 128, :] = both[:, 64:]

    for row in (2, 3):
        for pair in (1, 2):
            put(row, pair, poles[2 * (row - 2) + pair - 1])
    for side in range(2):

        @pl.when(place[0] == side)
        def _():
            for base, buffer in ((4 - 4 * side, paired_rows), (4 * side, across_rows)):
                for row in range(2):
                    for pair in (1, 2):
                        start = 128 * (2 * row + pair - 1)
                        put(base + row, pair, buffer[ROW_POLES:ROW_ALL, start : start + 128])

        @pl.when(place[1] == side)
        def _():
            for pair, buffer in ((3 - 3 * side, paired_cols), (3 * side, across_cols)):
                for row in range(6):
                    base, lane = COL_POLES + 32 * (row // 2), 256 * (row % 2)
                    put(row, pair, unflat(buffer[base : base + 32, lane : lane + 256]))

    low1, low2 = place[1] == 0, place[5] == 0
    for row in range(5):
        base, lane = 16 * (row // 2), 256 * (row % 2)
        pair_1 = paired_cols[COL_BOX + base : COL_BOX + base + 16, lane : lane + 256]
        across_1 = across_cols[COL_BOX + base : COL_BOX + base + 16, lane : lane + 256]
        pair_2, across_2 = [ref[base : base + 16, lane : lane + 256] for ref in (pair2, across2)]
        found = (
            jnp.where(low2, across_2, pair_2),
            jnp.where(low1, across_1, pair_1),
            boxes[base : base + 16, lane : lane + 256],
            jnp.where(low1, pair_1, across_1),
            jnp.where(low2, pair_2, across_2),
        )
        for col in range(5):
            start = 64 * (5 * row + col)
            window[start : start + 64, :] = unfold(unflat(found[col]))
    spread = flag_row(flags[...])
    for row in range(2):
        for col in range(4):
            leaf = 4 * row + col
            seen = jnp.concatenate([table[row + a, 64 * col : 64 * (col + 5), :] for a in range(5)], axis=0)
            local[leaf] = box_product(coupling[leaf], spread[leaf : leaf + 1], seen).astype(BF16)
    box_out[...] = box_product(box_coupling[0], spread[8:9], window[...])
    near_pairs(col_pairs(), mask_copy, mask, listed, feats, offs, charges, acc)
    for leaf in range(8):
        far = lax.dot_general(local[leaf], basis[leaf], TN, preferred_element_type=F32)
        out[leaf] = acc[leaf] + far


def last_kernel(
    near, box_one, flags, box_coupling, moved_basis,
    sums, pair2, across2, boxes3, pair4, across4, pair8,
    out_hbm, window, out, sems,
):
    place = place_bits()
    spread = flag_row(flags[...])
    total = box_one[...]
    low2, low4, low8 = place[5] == 0, place[6] == 0, place[7] == 0
    blank = jnp.zeros((16, 256), BF16)
    for level in range(2):
        lanes = slice(256 * level, 256 * level + 256)
        for row in range(5):
            rows = slice(16 * row, 16 * row + 16)
            later = slice(48 + 16 * row, 64 + 16 * row)
            pair_4, across_4 = pair4[rows, lanes], across4[rows, lanes]
            minus4, plus4 = jnp.where(low4, across_4, pair_4), jnp.where(low4, pair_4, across_4)
            if level == 0:
                pair_2, across_2 = pair2[later, lanes], across2[later, lanes]
                minus2, plus2 = jnp.where(low2, across_2, pair_2), jnp.where(low2, pair_2, across_2)
                found = (minus4, minus2, sums[rows, lanes], plus2, plus4)
            else:
                far = pair8[rows, :]
                found = (jnp.where(low8, blank, far), minus4, boxes3[rows, :], plus4, jnp.where(low8, far, blank))
            for col in range(5):
                start = 64 * (5 * row + col)
                window[start : start + 64, :] = unfold(unflat(found[col]))
        total = total + box_product(box_coupling[1 + level], spread[9 + level : 10 + level], window[...])
    total = total.T.astype(BF16)
    stores = [pltpu.make_async_copy(out.at[leaf], out_hbm.at[leaf], sems.at[leaf]) for leaf in range(8)]
    for leaf in range(8):
        far = jnp.dot(total, moved_basis[leaf], preferred_element_type=F32)
        out[leaf] = (near[leaf] + far).astype(BF16)
        stores[leaf].start()
    for store in stores:
        store.wait()


def near_scratch(sources):
    return [
        pltpu.SMEM((8, 8), jnp.int32),
        pltpu.SemaphoreType.DMA(()),
        pltpu.SMEM((32,), jnp.int32),
        pltpu.VMEM((8, 8, PANELS), F32),
        *([pltpu.VMEM((8, LOADS, PANELS), BF16)] if sources else []),
        pltpu.VMEM((8, LOADS, PANELS), F32),
    ]


def body(
    charges,
    offsets,
    leaf_basis,
    near_mask,
    leaf_coupling,
    leaf_distant_flags,
    leaf_transfer,
    box_coupling,
    box_far,
    parent_child_transfer,
):
    charges = charges.reshape(8, LOADS, PANELS)
    offsets = offsets.transpose(0, 2, 1, 3)
    basis = leaf_basis.reshape(8, RANK, PANELS)
    mask = near_mask.reshape(8, 8)
    coupling = leaf_coupling.reshape(8, RANK, WIDE)
    transfer = leaf_transfer.reshape(8, RANK, RANK)
    box_coupling = box_coupling.reshape(3, RANK, WIDE)
    parent = parent_child_transfer.reshape(2, RANK, RANK)
    flags = jnp.concatenate([leaf_distant_flags.reshape(8, 25), box_far.reshape(3, 25)], axis=0)
    flags = jnp.pad(flags, ((0, 5), (0, 7))).astype(BF16)
    near_cost = 6 * 10**9
    rows_pair, rows_across, small, poles, feats = kernel_call(
        first_kernel,
        (shape((ROW_ALL, 512)), shape((ROW_ALL, 512)), shape((3, 32, 128)), shape((4, 64, 128)), shape((8, PANELS, 16))),
        [
            pltpu.VMEM((8, LOADS, PANELS), BF16),
            pltpu.VMEM((2, 3, 4, PANELS), BF16),
            pltpu.VMEM((8, RANK, PANELS), BF16),
            pltpu.VMEM((8, RANK, RANK), BF16),
            pltpu.VMEM((2, RANK, RANK), BF16),
            pltpu.SemaphoreType.DMA((11,)),
        ],
        "first", 10**9, charges, offsets, basis, transfer, parent, hbm=(0, 1, 2, 3, 4),
    )

    pair1 = paired(small, "row", 1)
    paired_rows = paired(rows_pair, "row", 1)
    near_args = (mask, charges, offsets, feats)

    def inner_call(kernel, count, name, after):
        return kernel_call(
            kernel, shape((count, LOADS, PANELS), F32),
            near_scratch(False), name, near_cost, *near_args, after=after,
        )

    halves = (small[1:3].astype(F32) + pair1[1:3].astype(F32)).astype(BF16)
    payload = jnp.concatenate([small[:1], pair1[:1], halves], axis=0)
    pair2 = paired(payload, "row", 2)
    inner0 = inner_call(early_inner_kernel, 8, "inner0", (payload,))
    pair2, inner0 = lax.optimization_barrier((pair2, inner0))
    quarter = (small[2].astype(F32) + pair1[2].astype(F32) + pair2[3].astype(F32)).astype(BF16)
    payload = jnp.concatenate([pair2[2:3], quarter[None], small[:1], pair1[:1], halves[:1]], axis=0)
    pair4 = paired(payload, "row", 6)
    payload, rows_across = lax.optimization_barrier((payload, rows_across))
    across_rows = paired_across(rows_across, "row", 1)
    inner1 = inner_call(functools.partial(late_inner_kernel, (3, 4, 5), 1), 3, "inner1", (payload,))
    pair4, inner1 = lax.optimization_barrier((pair4, inner1))
    payload = jnp.concatenate([quarter[None], pair4[1:2], pair4[0:1], pair4[2:5]], axis=0)
    pair8, across8 = paired(payload, "row", 8), paired_across(payload, "row", 8)
    by_rows = kernel_call(
        row_kernel, shape((8, LOADS, PANELS), F32), near_scratch(True), "byrows", near_cost,
        mask, feats, paired_rows, across_rows, after=(payload,),
    )

    pair8, across8, by_rows = lax.optimization_barrier((pair8, across8, by_rows))

    cols_pair, cols_across, boxes1, row_sums = kernel_call(
        pack_kernel,
        (shape((COL_ALL + SUMS, 512)), shape((COL_ALL, 512)), shape((48, 512)), shape((SUMS, 512))),
        [], "pack", 10**8, charges, offsets, poles, paired_rows, across_rows,
        small, pair1, pair2, pair4, pair8, across8,
    )
    paired_cols = paired(cols_pair, "col", 1)
    across_cols = paired_across(cols_across, "col", 1)
    sums = (row_sums.astype(F32) + paired_cols[COL_ALL:].astype(F32)).astype(BF16)
    payload = jnp.concatenate([boxes1, sums], axis=0)
    col_pair2 = paired(payload, "col", 2)
    moved_basis = kernel_call(
        basis_kernel, shape((8, RANK, PANELS)), [], "basis", 10**8, transfer, basis, after=(payload,)
    )
    across_payload, moved_basis = lax.optimization_barrier((payload, moved_basis))
    col_across2 = paired_across(across_payload, "col", 2)
    inner2 = inner_call(functools.partial(late_inner_kernel, (6, 7), 2), 2, "inner2", (moved_basis,))
    col_pair2, inner2 = lax.optimization_barrier((col_pair2, inner2))
    boxes3 = (sums[:, 256:].astype(F32) + col_pair2[48:, 256:].astype(F32)).astype(BF16)
    payload = jnp.concatenate([sums[:, :256], boxes3], axis=1)
    col_pair4, col_across4 = paired(payload, "col", 4), paired_across(payload, "col", 4)
    col_pair8 = paired(boxes3, "col", 10)
    direct, box_one = kernel_call(
        edge_kernel,
        (shape((8, LOADS, PANELS), F32), shape((RANK, LOADS), F32)),
        near_scratch(True)
        + [pltpu.VMEM((6, 512, LOADS), BF16), pltpu.VMEM((WIDE, LOADS), BF16), pltpu.VMEM((8, RANK, LOADS), BF16)],
        "edge", near_cost, mask, feats, paired_cols, across_cols, inner0, inner1, inner2, by_rows, poles,
        paired_rows, across_rows, flags, coupling, box_coupling, boxes1, col_pair2, col_across2, basis,
        after=(payload,),
    )
    out = kernel_call(
        last_kernel, shape((8, LOADS, PANELS)),
        [pltpu.VMEM((WIDE, LOADS), BF16), pltpu.VMEM((8, LOADS, PANELS), BF16), pltpu.SemaphoreType.DMA((8,))], "last", 10**9,
        direct, box_one, flags, box_coupling, moved_basis,
        sums, col_pair2, col_across2, boxes3, col_pair4, col_across4, col_pair8, out_space=HBM,
    )
    return out.reshape(2, 4, LOADS, PANELS)


def solution(mesh):
    return jax.shard_map(
        body,
        mesh=mesh,
        in_specs=(
            P("row", "col", None, None),
            P("row", "col", None, None),
            P("row", "col", None, None),
            P("row", "col", None),
            P("row", "col", None, None),
            P("row", "col", None),
            P("row", "col", None, None),
            P("row", "col", None, None, None),
            P("row", "col", None, None),
            P("row", "col", None, None, None),
        ),
        out_specs=P("row", "col", None, None),
        check_vma=False,
    )
```

```python
import functools

import jax
import jax.numpy as jnp
from jax import lax
from jax.experimental import pallas as pl
from jax.experimental.pallas import tpu as pltpu
from jax.sharding import PartitionSpec as P

PANELS = 512
RANK = 64
LOADS = 64
EPSILON = 0.001
F32 = jnp.float32
BF16 = jnp.bfloat16
NT = (((1,), (1,)), ((), ()))
TN = (((0,), (0,)), ((), ()))
WIDE = 25 * RANK
MIB = 2**20
AT_ONCE = (8, 4, 2, 1)
VMEM = pl.BlockSpec(memory_space=pltpu.VMEM)
SMEM = pl.BlockSpec(memory_space=pltpu.SMEM)
HBM = pl.BlockSpec(memory_space=pltpu.HBM)

ROW_OFFS, ROW_POLES, ROW_ALL = 256, 272, 336
COL_OFFS, COL_POLES, COL_BOX, COL_ALL = 256, 272, 368, 416
SUMS = 80


def paired(value, axis, distance):
    return lax.ppermute(value, axis, [(i, i ^ distance) for i in range(lax.axis_size(axis))])


def paired_across(value, axis, distance):
    count = lax.axis_size(axis)
    moves = [(i, i + distance if i & distance else i - distance) for i in range(count)]
    return lax.ppermute(value, axis, [(i, j) for i, j in moves if 0 <= j < count])


def kernel_call(body, outs, scratch, name, cost, *args, smem=(), hbm=(), after=(), out_space=VMEM):
    count = len(args)

    def with_order(*refs):
        body(*refs[:count], *refs[count + len(after) :])

    spaces = [SMEM if i in smem else HBM if i in hbm else VMEM for i in range(count)]
    return pl.pallas_call(
        with_order,
        out_shape=outs,
        in_specs=spaces + [VMEM] * len(after),
        out_specs=jax.tree.map(lambda _: out_space, outs),
        scratch_shapes=scratch,
        compiler_params=pltpu.CompilerParams(vmem_limit_bytes=40 * MIB),
        cost_estimate=pl.CostEstimate(flops=cost, bytes_accessed=4 * MIB, transcendentals=0),
        name=name,
    )(*[pltpu.with_memory_space_constraint(arg, pltpu.HBM) if i in hbm else arg for i, arg in enumerate(args)], *after)


def shape(dims, dtype=BF16):
    return jax.ShapeDtypeStruct(dims, dtype)


def fold(matrix):
    return jnp.concatenate([matrix[:32], matrix[32:]], axis=1)


def unfold(folded):
    return jnp.concatenate([folded[:, :64], folded[:, 64:]], axis=0)


def place_bits():
    row, col = lax.axis_index("row"), lax.axis_index("col")
    return [value & 1 for value in (row, col, row >> 1, row >> 2, row >> 3, col >> 1, col >> 2, col >> 3)]


def flat(folded):
    return jnp.concatenate([folded[:16], folded[16:]], axis=1)


def unflat(flattened):
    return jnp.concatenate([flattened[:, :128], flattened[:, 128:]], axis=0)


def rows_of(values, count):
    row = lax.broadcasted_iota(jnp.int32, (count, PANELS), 0)
    out = jnp.zeros((count, PANELS), F32)
    for index, value in enumerate(values):
        out = jnp.where(row == index, value, out)
    return out


def three_parts(value):
    high = value.astype(BF16).astype(F32)
    rest = value - high
    middle = rest.astype(BF16).astype(F32)
    low = (rest - middle).astype(BF16).astype(F32)
    return high, middle, low


def target_features(off):
    x, y, z = off
    high, middle, low = three_parts(PANELS * (x * x + y * y + z * z + EPSILON))
    return rows_of([x, y, z, x, y, high, middle, low, 1.0, 1.0, 1.0], 16).T.astype(BF16)


def source_features(off, row_off, col_off):
    x, y, z = off[0:1], off[1:2], off[2:3]
    x_moved, y_moved = x + col_off, y + row_off
    high, middle, low = three_parts(PANELS * (x_moved * x_moved + y_moved * y_moved + z * z))
    twice = -2.0 * PANELS
    return rows_of(
        [twice * x, twice * y, twice * z, twice * col_off, twice * row_off, 1.0, 1.0, 1.0, high, middle, low], 16
    ).astype(BF16)


def near_pairs(pairs, mask_copy, mask, listed, target_feats, source_offs, source_charges, acc):
    mask_copy.wait()
    count = jnp.int32(0)
    for target, slot, source, row_off, col_off in pairs:
        listed[count] = target + 16 * source + 256 * (row_off + 1) + 1024 * (col_off + 1)
        count = count + (1 if slot is None else mask[target, slot])

    def one(index):
        code = listed[index]
        target = code & 15
        source = (code >> 4) & 15
        row_off = ((code >> 8) & 3) - 1
        col_off = ((code >> 10) & 3) - 1
        moved = source_features(source_offs[source, 0:3, :], row_off.astype(F32), col_off.astype(F32))
        squared = jnp.dot(target_feats[target], moved, preferred_element_type=F32)
        tile = lax.rsqrt(squared).astype(BF16)
        acc[target] += lax.dot_general(source_charges[source], tile, NT, preferred_element_type=F32)

    done = jnp.int32(0)
    for at_once in AT_ONCE:
        steps = (count - done) // at_once

        def several(step, carry, done=done, at_once=at_once):
            for k in range(at_once):
                one(done + step * at_once + k)
            return carry

        lax.fori_loop(0, steps, several, 0)
        done = done + steps * at_once


def slot_of(row_off, col_off):
    place = 3 * (row_off + 1) + col_off + 1
    return None if place == 4 else place - (place > 4)


def inner_pairs(targets):
    found = []
    for target in targets:
        row, col = divmod(target, 4)
        for row_off in (-1, 0, 1):
            for col_off in (-1, 0, 1):
                at_row, at_col = row + row_off, col + col_off
                if 0 <= at_row < 2 and 0 <= at_col < 4:
                    found.append((target, slot_of(row_off, col_off), 4 * at_row + at_col, row_off, col_off))
    return found


def row_pairs():
    found = []
    for row, row_off in ((0, -1), (1, 1)):
        for col in range(4):
            for col_off in (-1, 0, 1):
                if 0 <= col + col_off < 4:
                    found.append((4 * row + col, slot_of(row_off, col_off), 4 * row + col + col_off, row_off, col_off))
    return found


def col_pairs():
    found = []
    for side, col, col_off in ((0, 0, -1), (1, 3, 1)):
        for row in range(2):
            for row_off in (-1, 0, 1):
                found.append((4 * row + col, slot_of(row_off, col_off), 4 * side + row + row_off + 1, row_off, col_off))
    return found


def first_kernel(
    charges_hbm, offsets_hbm, basis_hbm, transfer_hbm, parent_hbm,
    with_pair, across, small, poles_out, feats,
    charges, offsets, basis, transfer, parent, sems,
):
    side = place_bits()[0]
    loads = []
    for k in range(4):
        rows = pl.ds(2 * k, 2)
        loads.append(pltpu.make_async_copy(charges_hbm.at[rows], charges.at[rows], sems.at[k]))
        loads.append(pltpu.make_async_copy(basis_hbm.at[rows], basis.at[rows], sems.at[4 + k]))
    loads.append(pltpu.make_async_copy(transfer_hbm, transfer, sems.at[8]))
    loads.append(pltpu.make_async_copy(parent_hbm, parent, sems.at[9]))
    load_offsets = pltpu.make_async_copy(offsets_hbm, offsets, sems.at[10])
    load_offsets.start()
    for load in loads:
        load.start()
    load_offsets.wait()
    offs = [[offsets[row, k].astype(F32) for k in range(3)] for row in range(2)]
    halves = [rows_of([offs[row][k % 3][k // 3 : k // 3 + 1] for k in range(12)], 16).astype(BF16) for row in range(2)]
    with_pair[ROW_OFFS:ROW_POLES, :] = jnp.where(side == 0, halves[1], halves[0])
    across[ROW_OFFS:ROW_POLES, :] = jnp.where(side == 0, halves[0], halves[1])
    for leaf in range(8):
        row, col = divmod(leaf, 4)
        feats[leaf] = target_features([offs[row][k][col : col + 1] for k in range(3)])
    poles = []
    for k in range(4):
        loads[2 * k].wait()
        loads[2 * k + 1].wait()
        for leaf in (2 * k, 2 * k + 1):
            poles.append(lax.dot_general(basis[leaf], charges[leaf], NT, preferred_element_type=F32).astype(BF16))
    loads[8].wait()
    box = jnp.zeros((RANK, LOADS), F32)
    for leaf in range(8):
        box = box + lax.dot_general(transfer[leaf], poles[leaf], TN, preferred_element_type=F32)
    box = box.astype(BF16)
    small[0] = fold(box)
    loads[9].wait()
    for level in range(2):
        term = lax.dot_general(parent[level], box, TN, preferred_element_type=F32)
        small[1 + level] = fold(term.astype(BF16))
    pairs = [jnp.concatenate([poles[2 * k], poles[2 * k + 1]], axis=1) for k in range(4)]
    for k in range(4):
        poles_out[k] = pairs[k]
    for buffer, row in ((with_pair, 1 - side), (across, side)):
        for col in range(4):
            buffer[64 * col : 64 * (col + 1), :] = charges[4 * row + col]
        for k in range(4):
            buffer[ROW_POLES:ROW_ALL, 128 * k : 128 * (k + 1)] = pairs[k]


def own_offsets(offsets, offs):
    for row in range(2):
        for k in range(3):
            values = offsets[row, k].astype(F32)
            for col in range(4):
                offs[4 * row + col, k : k + 1, :] = values[col : col + 1]


def inner_kernel(targets, mask_in, charges, offsets, feats, out, mask, sem, listed, offs, acc):
    mask_copy = pltpu.make_async_copy(mask_in, mask, sem)
    mask_copy.start()
    own_offsets(offsets, offs)
    for target in targets:
        acc[target] = jnp.zeros((LOADS, PANELS), F32)
    near_pairs(inner_pairs(targets), mask_copy, mask, listed, feats, offs, charges, acc)
    out[...] = acc[targets[0] : targets[-1] + 1]


def earliness():
    row = lax.axis_index("row")
    return jnp.where(row & 7 == 0, 2, jnp.where(row & 4 == 0, 1, 0))


def early_inner_kernel(mask_in, charges, offsets, feats, out, *scratch):
    ahead = earliness()
    for count, targets in enumerate(((0, 1, 2), (0, 1, 2, 3, 4, 5), (0, 1, 2, 3, 4, 5, 6, 7))):

        @pl.when(ahead == count)
        def _():
            inner_kernel(targets, mask_in, charges, offsets, feats, out.at[0 : len(targets)], *scratch)


def late_inner_kernel(targets, limit, *refs):
    @pl.when(earliness() < limit)
    def _():
        inner_kernel(targets, *refs)


def basis_kernel(start, transfer, basis, out):
    for leaf in range(4):
        moved = lax.dot_general(transfer[start + leaf], basis[start + leaf], TN, preferred_element_type=F32)
        out[leaf] = moved.astype(BF16)


def spread_offsets(packed, offs, base):
    values = packed.astype(F32)
    for leaf in range(4):
        offs[base + leaf, 0:3, :] = values[3 * leaf : 3 * leaf + 3]


def row_kernel(mask_in, feats, paired_rows, across_rows, out, mask, sem, listed, offs, charges, acc):
    mask_copy = pltpu.make_async_copy(mask_in, mask, sem)
    mask_copy.start()
    place = place_bits()
    for side, buffer in ((1 - place[0], paired_rows), (place[0], across_rows)):
        spread_offsets(buffer[ROW_OFFS:ROW_POLES, :], offs, 4 * side)
        for col in range(4):
            charges[4 * side + col] = buffer[64 * col : 64 * (col + 1), :]
    acc[...] = jnp.zeros_like(acc)
    near_pairs(row_pairs(), mask_copy, mask, listed, feats, offs, charges, acc)
    out[...] = acc[...]


def pack_kernel(
    charges, offsets, poles, paired_rows, across_rows, small, pair1, pair2, pair4, pair8, across8,
    with_pair, across, boxes_out, sums_out,
):
    place = place_bits()
    bit0, bit1, bit2 = place[0], place[2], place[3]
    at = bit0 == 0
    minus8, plus8 = [[jnp.where(place[4] == want, pair8[k], across8[k]) for k in range(6)] for want in (1, 0)]
    low2, low4 = bit1 == 0, bit2 == 0
    minus2, plus2 = [], []
    for k in range(3):
        other = jnp.where(low2 != low4, pair4[2 + k], jnp.where(low2, minus8[3 + k], plus8[3 + k]))
        minus2.append(jnp.where(low2, other, pair2[k]))
        plus2.append(jnp.where(low2, pair2[k], other))
    boxes = [
        minus2[0],
        jnp.where(at, minus2[1], pair1[0]),
        small[0],
        jnp.where(at, pair1[0], plus2[1]),
        plus2[0],
    ]
    own2 = (small[1].astype(F32) + pair1[1].astype(F32)).astype(BF16)
    own3 = (small[2].astype(F32) + pair1[2].astype(F32) + pair2[3].astype(F32)).astype(BF16)
    second = [
        jnp.where(low4, minus8[2], pair4[0]),
        minus2[2],
        own2,
        plus2[2],
        jnp.where(low4, pair4[0], plus8[2]),
    ]
    third = [
        minus8[0],
        jnp.where(low4, minus8[1], pair4[1]),
        own3,
        jnp.where(low4, pair4[1], plus8[1]),
        plus8[0],
    ]
    for row in range(5):
        base, lane = 16 * (row // 2), 256 * (row % 2)
        piece = flat(boxes[row])
        boxes_out[base : base + 16, lane : lane + 256] = piece
        for buffer in (with_pair, across):
            buffer[COL_BOX + base : COL_BOX + base + 16, lane : lane + 256] = piece
        for half, found in enumerate((second, third)):
            piece = flat(found[row])
            sums_out[16 * row : 16 * row + 16, 256 * half : 256 * half + 256] = piece
            with_pair[COL_ALL + 16 * row : COL_ALL + 16 * row + 16, 256 * half : 256 * half + 256] = piece
    blank = jnp.zeros((16, 256), BF16)
    boxes_out[32:48, 256:512] = blank
    for buffer in (with_pair, across):
        buffer[COL_BOX + 32 : COL_ALL, 256:512] = blank

    def fill(buffer, col, top, bottom):
        pair = col // 2
        offs = []
        for spot, source in enumerate((top, None, None, bottom)):
            if source is None:
                leaf = 4 * (spot - 1) + col
                buffer[64 * spot : 64 * (spot + 1), :] = charges[leaf]
                offs += [offsets[spot - 1, k].astype(F32)[col : col + 1] for k in range(3)]
            else:
                buffer[64 * spot : 64 * (spot + 1), :] = source[64 * col : 64 * (col + 1), :]
                off = source[ROW_OFFS:ROW_POLES, :].astype(F32)[3 * col : 3 * col + 3]
                offs += [off[0:1], off[1:2], off[2:3]]
        buffer[COL_OFFS:COL_POLES, :] = rows_of(offs, 16).astype(BF16)
        for row in range(6):
            if row in (2, 3):
                pole = poles[2 * (row - 2) + pair]
            else:
                source = top if row < 2 else bottom
                start = 128 * (2 * (row % 4) + pair)
                pole = source[ROW_POLES:ROW_ALL, start : start + 128]
            base, lane = COL_POLES + 32 * (row // 2), 256 * (row % 2)
            buffer[base : base + 32, lane : lane + 128] = pole[:32]
            buffer[base : base + 32, lane + 128 : lane + 256] = pole[32:]

    for row_side in range(2):
        for col_side in range(2):

            @pl.when((place[0] == row_side) & (place[1] == col_side))
            def _():
                top, bottom = (across_rows, paired_rows) if row_side == 0 else (paired_rows, across_rows)
                fill(with_pair, 0 if col_side else 3, top, bottom)
                fill(across, 3 if col_side else 0, top, bottom)


def flag_row(flags):
    row = lax.broadcasted_iota(jnp.int32, (32, WIDE), 0)
    lane = lax.broadcasted_iota(jnp.int32, (32, WIDE), 1)
    spread = jnp.where((lane >> 6) == row, 1.0, 0.0).astype(BF16)
    return jnp.dot(flags, spread, preferred_element_type=F32).astype(BF16)


def box_product(coupling, flags, window):
    return jnp.dot(coupling * flags, window, preferred_element_type=F32)


def edge_kernel(
    mask_in, feats, paired_cols, across_cols, inner0, inner1, inner2, by_rows, poles, paired_rows, across_rows, flags, coupling,
    box_coupling, boxes, pair2, across2, basis,
    out, box_out, mask, sem, listed, offs, charges, acc, table, window, local,
):
    mask_copy = pltpu.make_async_copy(mask_in, mask, sem)
    mask_copy.start()
    place = place_bits()
    for side, buffer in ((1 - place[1], paired_cols), (place[1], across_cols)):
        spread_offsets(buffer[COL_OFFS:COL_POLES, :], offs, 4 * side)
        for spot in range(4):
            charges[4 * side + spot] = buffer[64 * spot : 64 * (spot + 1), :]
    acc[0:3] = inner0[0:3] + by_rows[0:3]

    for first, last, late, limit in ((3, 6, inner1, 1), (6, 8, inner2, 2)):

        @pl.when(earliness() >= limit)
        def _():
            acc[first:last] = inner0[first:last] + by_rows[first:last]

        @pl.when(earliness() < limit)
        def _():
            acc[first:last] = late[...] + by_rows[first:last]


    def put(row, pair, both):
        table[row, 128 * pair : 128 * pair + 64, :] = both[:, :64]
        table[row, 128 * pair + 64 : 128 * pair + 128, :] = both[:, 64:]

    for row in (2, 3):
        for pair in (1, 2):
            put(row, pair, poles[2 * (row - 2) + pair - 1])
    for side in range(2):

        @pl.when(place[0] == side)
        def _():
            for base, buffer in ((4 - 4 * side, paired_rows), (4 * side, across_rows)):
                for row in range(2):
                    for pair in (1, 2):
                        start = 128 * (2 * row + pair - 1)
                        put(base + row, pair, buffer[ROW_POLES:ROW_ALL, start : start + 128])

        @pl.when(place[1] == side)
        def _():
            for pair, buffer in ((3 - 3 * side, paired_cols), (3 * side, across_cols)):
                for row in range(6):
                    base, lane = COL_POLES + 32 * (row // 2), 256 * (row % 2)
                    put(row, pair, unflat(buffer[base : base + 32, lane : lane + 256]))

    low1, low2 = place[1] == 0, place[5] == 0
    for row in range(5):
        base, lane = 16 * (row // 2), 256 * (row % 2)
        pair_1 = paired_cols[COL_BOX + base : COL_BOX + base + 16, lane : lane + 256]
        across_1 = across_cols[COL_BOX + base : COL_BOX + base + 16, lane : lane + 256]
        pair_2, across_2 = [ref[base : base + 16, lane : lane + 256] for ref in (pair2, across2)]
        found = (
            jnp.where(low2, across_2, pair_2),
            jnp.where(low1, across_1, pair_1),
            boxes[base : base + 16, lane : lane + 256],
            jnp.where(low1, pair_1, across_1),
            jnp.where(low2, pair_2, across_2),
        )
        for col in range(5):
            start = 64 * (5 * row + col)
            window[start : start + 64, :] = unfold(unflat(found[col]))
    spread = flag_row(flags[...])
    for row in range(2):
        for col in range(4):
            leaf = 4 * row + col
            seen = jnp.concatenate([table[row + a, 64 * col : 64 * (col + 5), :] for a in range(5)], axis=0)
            local[leaf] = box_product(coupling[leaf], spread[leaf : leaf + 1], seen).astype(BF16)
    box_out[...] = box_product(box_coupling[0], spread[8:9], window[...])
    near_pairs(col_pairs(), mask_copy, mask, listed, feats, offs, charges, acc)
    for leaf in range(8):
        far = lax.dot_general(local[leaf], basis[leaf], TN, preferred_element_type=F32)
        out[leaf] = acc[leaf] + far


def last_kernel(
    near, box_one, flags, box_coupling, basis0, basis4,
    sums, pair2, across2, boxes3, pair4, across4, pair8,
    out_hbm, window, out, sems,
):
    place = place_bits()
    spread = flag_row(flags[...])
    total = box_one[...]
    low2, low4, low8 = place[5] == 0, place[6] == 0, place[7] == 0
    blank = jnp.zeros((16, 256), BF16)
    for level in range(2):
        lanes = slice(256 * level, 256 * level + 256)
        for row in range(5):
            rows = slice(16 * row, 16 * row + 16)
            later = slice(48 + 16 * row, 64 + 16 * row)
            pair_4, across_4 = pair4[rows, lanes], across4[rows, lanes]
            minus4, plus4 = jnp.where(low4, across_4, pair_4), jnp.where(low4, pair_4, across_4)
            if level == 0:
                pair_2, across_2 = pair2[later, lanes], across2[later, lanes]
                minus2, plus2 = jnp.where(low2, across_2, pair_2), jnp.where(low2, pair_2, across_2)
                found = (minus4, minus2, sums[rows, lanes], plus2, plus4)
            else:
                far = pair8[rows, :]
                found = (jnp.where(low8, blank, far), minus4, boxes3[rows, :], plus4, jnp.where(low8, far, blank))
            for col in range(5):
                start = 64 * (5 * row + col)
                window[start : start + 64, :] = unfold(unflat(found[col]))
        total = total + box_product(box_coupling[1 + level], spread[9 + level : 10 + level], window[...])
    total = total.T.astype(BF16)
    stores = [pltpu.make_async_copy(out.at[leaf], out_hbm.at[leaf], sems.at[leaf]) for leaf in range(8)]
    for leaf in range(8):
        far = jnp.dot(total, (basis0 if leaf < 4 else basis4)[leaf % 4], preferred_element_type=F32)
        out[leaf] = (near[leaf] + far).astype(BF16)
        stores[leaf].start()
    for store in stores:
        store.wait()


def near_scratch(sources):
    return [
        pltpu.SMEM((8, 8), jnp.int32),
        pltpu.SemaphoreType.DMA(()),
        pltpu.SMEM((32,), jnp.int32),
        pltpu.VMEM((8, 8, PANELS), F32),
        *([pltpu.VMEM((8, LOADS, PANELS), BF16)] if sources else []),
        pltpu.VMEM((8, LOADS, PANELS), F32),
    ]


def body(
    charges,
    offsets,
    leaf_basis,
    near_mask,
    leaf_coupling,
    leaf_distant_flags,
    leaf_transfer,
    box_coupling,
    box_far,
    parent_child_transfer,
):
    charges = charges.reshape(8, LOADS, PANELS)
    offsets = offsets.transpose(0, 2, 1, 3)
    basis = leaf_basis.reshape(8, RANK, PANELS)
    mask = near_mask.reshape(8, 8)
    coupling = leaf_coupling.reshape(8, RANK, WIDE)
    transfer = leaf_transfer.reshape(8, RANK, RANK)
    box_coupling = box_coupling.reshape(3, RANK, WIDE)
    parent = parent_child_transfer.reshape(2, RANK, RANK)
    flags = jnp.concatenate([leaf_distant_flags.reshape(8, 25), box_far.reshape(3, 25)], axis=0)
    flags = jnp.pad(flags, ((0, 5), (0, 7))).astype(BF16)
    near_cost = 6 * 10**9
    rows_pair, rows_across, small, poles, feats = kernel_call(
        first_kernel,
        (shape((ROW_ALL, 512)), shape((ROW_ALL, 512)), shape((3, 32, 128)), shape((4, 64, 128)), shape((8, PANELS, 16))),
        [
            pltpu.VMEM((8, LOADS, PANELS), BF16),
            pltpu.VMEM((2, 3, 4, PANELS), BF16),
            pltpu.VMEM((8, RANK, PANELS), BF16),
            pltpu.VMEM((8, RANK, RANK), BF16),
            pltpu.VMEM((2, RANK, RANK), BF16),
            pltpu.SemaphoreType.DMA((11,)),
        ],
        "first", 10**9, charges, offsets, basis, transfer, parent, hbm=(0, 1, 2, 3, 4),
    )

    pair1 = paired(small, "row", 1)
    paired_rows = paired(rows_pair, "row", 1)
    near_args = (mask, charges, offsets, feats)

    def inner_call(kernel, count, name, after):
        return kernel_call(
            kernel, shape((count, LOADS, PANELS), F32),
            near_scratch(False), name, near_cost, *near_args, after=after,
        )

    halves = (small[1:3].astype(F32) + pair1[1:3].astype(F32)).astype(BF16)
    payload = jnp.concatenate([small[:1], pair1[:1], halves], axis=0)
    pair2 = paired(payload, "row", 2)
    inner0 = inner_call(early_inner_kernel, 8, "inner0", (payload,))
    pair2, inner0 = lax.optimization_barrier((pair2, inner0))
    quarter = (small[2].astype(F32) + pair1[2].astype(F32) + pair2[3].astype(F32)).astype(BF16)
    payload = jnp.concatenate([pair2[2:3], quarter[None], small[:1], pair1[:1], halves[:1]], axis=0)
    pair4 = paired(payload, "row", 6)
    payload, rows_across = lax.optimization_barrier((payload, rows_across))
    across_rows = paired_across(rows_across, "row", 1)
    inner1 = inner_call(functools.partial(late_inner_kernel, (3, 4, 5), 1), 3, "inner1", (payload,))
    pair4, inner1 = lax.optimization_barrier((pair4, inner1))
    payload = jnp.concatenate([quarter[None], pair4[1:2], pair4[0:1], pair4[2:5]], axis=0)
    pair8, across8 = paired(payload, "row", 8), paired_across(payload, "row", 8)
    by_rows = kernel_call(
        row_kernel, shape((8, LOADS, PANELS), F32), near_scratch(True), "byrows", near_cost,
        mask, feats, paired_rows, across_rows, after=(payload,),
    )

    pair8, across8, by_rows = lax.optimization_barrier((pair8, across8, by_rows))

    cols_pair, cols_across, boxes1, row_sums = kernel_call(
        pack_kernel,
        (shape((COL_ALL + SUMS, 512)), shape((COL_ALL, 512)), shape((48, 512)), shape((SUMS, 512))),
        [], "pack", 10**8, charges, offsets, poles, paired_rows, across_rows,
        small, pair1, pair2, pair4, pair8, across8,
    )
    paired_cols = paired(cols_pair, "col", 1)
    across_cols = paired_across(cols_across, "col", 1)
    sums = (row_sums.astype(F32) + paired_cols[COL_ALL:].astype(F32)).astype(BF16)
    payload = jnp.concatenate([boxes1, sums], axis=0)
    col_pair2 = paired(payload, "col", 2)
    def basis_call(start, after):
        return kernel_call(
            functools.partial(basis_kernel, start), shape((4, RANK, PANELS)), [], f"basis{start}", 10**8,
            transfer, basis, after=after,
        )

    basis0 = basis_call(0, (payload,))
    across_payload, basis0 = lax.optimization_barrier((payload, basis0))
    col_across2 = paired_across(across_payload, "col", 2)
    inner2 = inner_call(functools.partial(late_inner_kernel, (6, 7), 2), 2, "inner2", (basis0,))
    col_pair2, inner2 = lax.optimization_barrier((col_pair2, inner2))
    boxes3 = (sums[:, 256:].astype(F32) + col_pair2[48:, 256:].astype(F32)).astype(BF16)
    payload = jnp.concatenate([sums[:, :256], boxes3], axis=1)
    col_pair4 = paired(payload, "col", 4)
    col_pair8 = paired(boxes3, "col", 10)
    basis4 = basis_call(4, (payload,))
    across_payload, basis4 = lax.optimization_barrier((payload, basis4))
    col_across4 = paired_across(across_payload, "col", 4)
    direct, box_one = kernel_call(
        edge_kernel,
        (shape((8, LOADS, PANELS), F32), shape((RANK, LOADS), F32)),
        near_scratch(True)
        + [pltpu.VMEM((6, 512, LOADS), BF16), pltpu.VMEM((WIDE, LOADS), BF16), pltpu.VMEM((8, RANK, LOADS), BF16)],
        "edge", near_cost, mask, feats, paired_cols, across_cols, inner0, inner1, inner2, by_rows, poles,
        paired_rows, across_rows, flags, coupling, box_coupling, boxes1, col_pair2, col_across2, basis,
        after=(across_payload,),
    )
    out = kernel_call(
        last_kernel, shape((8, LOADS, PANELS)),
        [pltpu.VMEM((WIDE, LOADS), BF16), pltpu.VMEM((8, LOADS, PANELS), BF16), pltpu.SemaphoreType.DMA((8,))], "last", 10**9,
        direct, box_one, flags, box_coupling, basis0, basis4,
        sums, col_pair2, col_across2, boxes3, col_pair4, col_across4, col_pair8, out_space=HBM,
    )
    return out.reshape(2, 4, LOADS, PANELS)


def solution(mesh):
    return jax.shard_map(
        body,
        mesh=mesh,
        in_specs=(
            P("row", "col", None, None),
            P("row", "col", None, None),
            P("row", "col", None, None),
            P("row", "col", None),
            P("row", "col", None, None),
            P("row", "col", None),
            P("row", "col", None, None),
            P("row", "col", None, None, None),
            P("row", "col", None, None),
            P("row", "col", None, None, None),
        ),
        out_specs=P("row", "col", None, None),
        check_vma=False,
    )
```
